128 devices in a mesh: grp: 4 (over y), shard: 32 (over x, z, core).
Axes of the slice: x: 4, y: 4, z: 4, core: 2. Of those that a mesh axis runs over, the one named last changes fastest.
Arguments:
- new_rows: bfloat16 [32768, 1024], P(('grp', 'shard'))
- cluster_ids: int32 [32768], P(('grp', 'shard')), may hold values from 0 to 7, as said below
- new_order: int32 [32768], P(('grp', 'shard')), may hold values from 0 to 2147483646
- codes: bfloat16 [8, 8192, 1024], P('grp', 'shard'), may hold values from -8 to 8
- scales: float32 [8, 1024], P('grp')
- offsets: float32 [8, 1024], P('grp')
- counts: int32 [8], P('grp'), may hold values from 1024 to 8192, as said below
- earlier_order: int32 [8, 8192], P('grp', 'shard'), may hold values from 1 to 2147483646
Outputs:
- max_similarity: float32 [32768], P(('grp', 'shard'))
The draws below stay inside these ranges and needn't reach their ends.
Inputs may be any that keep to these rules, and one draw needn't show every extreme that they name: `cluster_ids`: in each device's block of 256 rows, no group's clusters are named by more than 128 rows, and some group's clusters are named by exactly 128 rows. `counts`: some cluster has all 8192 slots live.
All inputs are finite; a program needn't handle non-finite values.
Results may differ from the reference program's by a relative error of at most 0.00047.
Values may be sent and summed in bfloat16 or wider, within the bound.
A program may use at most 128 MiB of HBM per device.

```python
import math
import jax
import jax.numpy as jnp
from jax import lax

D = 1024
CLG = 2
NEW_DEV = 256
GROUPS = 4
SHARDS = 32
CLUSTERS = 8
ROWS_CL = 8192
NEW_TOTAL = 32768


def code_row(key, flat):
    inner = jax.random.fold_in(key, flat)
    row_scale = jnp.exp(jax.random.uniform(jax.random.fold_in(inner, 2), (), jnp.float32, math.log(0.25), math.log(2.0)))
    values = jnp.clip(jax.random.normal(jax.random.fold_in(inner, 1), (D,), jnp.float32), -4.0, 4.0)
    return values * row_scale


def scales_for(key):
    inner = jax.random.fold_in(key, 12)
    low, high = (math.log(0.3), math.log(3.0))
    return jnp.exp(jax.random.uniform(inner, (CLUSTERS, D), jnp.float32, low, high))


def offsets_for(key):
    inner = jax.random.fold_in(key, 13)
    return 0.5 * jax.random.normal(inner, (CLUSTERS, D), jnp.float32)


def row_groups(key):
    blocks = GROUPS * SHARDS
    half = NEW_DEV // 2
    full = jax.random.randint(jax.random.fold_in(key, 1), (SHARDS,), 0, GROUPS)
    owner = jnp.tile(full, GROUPS)
    other = (owner[:, None] + 1 + jax.random.randint(jax.random.fold_in(key, 2), (blocks, NEW_DEV - half), 0, GROUPS - 1)) % GROUPS
    merged = jnp.concatenate([jnp.broadcast_to(owner[:, None], (blocks, half)), other], axis=1)
    shuffle_key = jax.random.fold_in(key, 3)
    orders = jax.vmap(lambda block: jax.random.permutation(jax.random.fold_in(shuffle_key, block), NEW_DEV))(jnp.arange(blocks))
    return jnp.take_along_axis(merged, orders, axis=1).reshape(-1)


def ids_for(key):
    groups_of = row_groups(jax.random.fold_in(key, 21))
    within = jax.random.randint(jax.random.fold_in(key, 22), (NEW_TOTAL,), 0, CLG)
    return (groups_of * CLG + within).astype(jnp.int32)


def counts_for(key):
    values = jax.random.randint(jax.random.fold_in(key, 31), (CLUSTERS,), ROWS_CL // 8, ROWS_CL + 1)
    chosen = jax.random.randint(jax.random.fold_in(key, 32), (), 0, CLUSTERS)
    return values.at[chosen].set(ROWS_CL).astype(jnp.int32)


def draw_cluster_ids(key, part):
    return ids_for(key)


def draw_counts(key, part):
    return counts_for(key)


def draw_new_order(key, part):
    values = jax.random.randint(jax.random.fold_in(key, 51), (NEW_TOTAL,), 1, 2147483647)
    start_mark = jax.random.randint(jax.random.fold_in(key, 52), (NEW_TOTAL,), 0, 16)
    return jnp.where(start_mark == 0, 0, values).astype(jnp.int32)


def draw_codes(key, part):
    code_key = jax.random.fold_in(key, 11)
    flat = jnp.arange(CLUSTERS * ROWS_CL, dtype=jnp.int32)
    return jax.vmap(lambda item: code_row(code_key, item))(flat).reshape(CLUSTERS, ROWS_CL, D).astype(jnp.bfloat16)


def draw_scales(key, part):
    return scales_for(key)


def draw_offsets(key, part):
    return offsets_for(key)


def draw_new_rows(key, part):
    ids = ids_for(key)
    live = counts_for(key)
    target = jax.random.randint(jax.random.fold_in(key, 41), (NEW_TOTAL,), 0, live[ids])
    code_key = jax.random.fold_in(key, 11)
    source = jax.vmap(lambda item: code_row(code_key, item))(ids * ROWS_CL + target)
    clean = source * scales_for(key)[ids] + offsets_for(key)[ids]
    magnitude = jnp.sqrt(jnp.mean(clean * clean, axis=1, keepdims=True))
    spread = jnp.exp(jax.random.uniform(jax.random.fold_in(key, 42), (NEW_TOTAL, 1), jnp.float32, math.log(0.2), math.log(3.0)))
    noise = jax.random.normal(jax.random.fold_in(key, 43), (NEW_TOTAL, D), jnp.float32)
    return (clean + noise * magnitude * spread).astype(jnp.bfloat16)


def with_ends(values, own_key, smallest, top_value):
    shape = values.shape
    place = [jax.random.randint(jax.random.fold_in(own_key, axis), (), 0, shape[axis]) for axis in range(len(shape))]
    values = values.at[tuple(place)].set(smallest)
    longest = shape.index(max(shape))
    place[longest] = (place[longest] + 1) % shape[longest]
    return values.at[tuple(place)].set(top_value)


def setup_inputs(seed: int = 0) -> dict:
    key_of = jax.random.split(jax.random.key(seed), 9)
    return {
        "new_rows": draw_new_rows(jax.random.fold_in(key_of[8], 71), 0),
        "cluster_ids": draw_cluster_ids(jax.random.fold_in(key_of[8], 71), 0),
        "new_order": draw_new_order(jax.random.fold_in(key_of[8], 71), 0),
        "codes": draw_codes(jax.random.fold_in(key_of[8], 71), 0),
        "scales": draw_scales(jax.random.fold_in(key_of[8], 71), 0),
        "offsets": draw_offsets(jax.random.fold_in(key_of[8], 71), 0),
        "counts": draw_counts(jax.random.fold_in(key_of[8], 71), 0),
        "earlier_order": with_ends(jax.random.randint(key_of[7], (CLUSTERS, ROWS_CL), 1, 2147483647), jax.random.fold_in(key_of[7], 1), 1, 2147483646).astype(jnp.int32),
    }


epsilon = 1e-06

def unit_rows(values):
    return (values / jnp.sqrt(lax.optimization_barrier(jnp.sum(values * values, axis=-1, keepdims=True)) + epsilon)).astype(jnp.bfloat16)

def decode_cluster(packed):
    code_rows, scale_row, offset_row = packed
    return unit_rows(code_rows.astype(jnp.float32) * scale_row[None, :] + offset_row[None, :])

def reference(new_rows, cluster_ids, new_order, codes, scales, offsets, counts, earlier_order):
    queries = unit_rows(new_rows.astype(jnp.float32))
    row_total = queries.shape[0]
    key_units = lax.map(decode_cluster, (codes, scales, offsets))
    slot_ids = jnp.arange(ROWS_CL, dtype=jnp.int32)
    sorter = jnp.argsort(cluster_ids, stable=True).astype(jnp.int32)
    sorted_ids = cluster_ids[sorter]
    tile_len = math.gcd(row_total, 256)

    def one_tile(tile_num):
        begin = (tile_num * tile_len).astype(jnp.int32)
        picked = lax.dynamic_slice_in_dim(sorter, begin, tile_len)
        tile_ids = lax.dynamic_slice_in_dim(sorted_ids, begin, tile_len)
        tile_rows = queries[picked]
        tile_order = new_order[picked]

        def visit(cluster, running):
            cluster_keys = lax.dynamic_index_in_dim(key_units, cluster, 0, keepdims=False)
            cluster_order = lax.dynamic_index_in_dim(earlier_order, cluster, 0, keepdims=False)
            live_count = lax.dynamic_index_in_dim(counts, cluster, 0, keepdims=False)
            scores = jnp.dot(tile_rows, cluster_keys.T, preferred_element_type=jnp.float32)
            allowed = (tile_ids[:, None] == cluster) & (slot_ids[None, :] < live_count) & (cluster_order[None, :] < tile_order[:, None])
            return jnp.maximum(running, lax.optimization_barrier(jnp.max(jnp.where(allowed, scores, -1.0), axis=1)))
        return lax.fori_loop(tile_ids[0], tile_ids[tile_len - 1] + 1, visit, jnp.zeros((tile_len,), jnp.float32))
    sorted_best = lax.map(one_tile, jnp.arange(row_total // tile_len, dtype=jnp.int32)).reshape(row_total)
    return jnp.zeros((row_total,), jnp.float32).at[sorter].set(sorted_best)
```

```python
import functools

import jax
import jax.numpy as jnp
from jax import lax
from jax.experimental import pallas as pl
from jax.experimental.pallas import tpu as pltpu
from jax.sharding import PartitionSpec as P

MESH = pl.DeviceIdType.MESH
epsilon = 1e-06
DEAD = 2147483647
CH = 128

Q_ORDER = [
    (0, 0), (0, 3),
    (3, 0), (1, 0),
    (0, 1), (0, 2),
    (3, 3), (1, 3),
    (3, 1), (1, 1),
    (3, 2), (1, 2),
    (2, 0), (2, 3),
    (2, 1), (2, 2),
]
Q_SLOT = {place: i for i, place in enumerate(Q_ORDER)}
K_ORDER = [
    (0, 0, 0), (0, 0, 1), (0, 1, 0), (0, 1, 1),
    (0, 0, 2), (0, 0, 3), (0, 1, 2), (0, 1, 3),
]
J_ORDER = [0, 2, 1, 3]
for _j in J_ORDER:
    K_ORDER += [(3, 0, _j), (3, 1, _j), (1, 0, _j), (1, 1, _j)]
for _j in (0, 2):
    K_ORDER += [(2, 0, _j), (2, 1, _j), (2, 0, _j + 1), (2, 1, _j + 1)]
K_SLOT = {place: i for i, place in enumerate(K_ORDER)}
DY_ORDER = [0, 3, 1, 2]


def kernel(
    rows_hbm, ids_ref, order_ref, codes_hbm, scales_ref, offsets_ref, counts_ref, key_order_ref,
    out_ref,
    rows, codes, sendq, sendo, qbuf, kbuf, qord, kord, kob, acc, ans, perm,
    local_sem, send_sem, q_sem, k_sem, o_sem,
):
    y = lax.axis_index("grp")
    shard = lax.axis_index("shard")
    x, z, c = shard // 8, (shard // 2) % 4, shard % 2

    def device(dx=0, dy=0, dz=0, dc=0):
        return (
            (y + dy) % 4,
            (((x + dx) % 4) * 4 + (z + dz) % 4) * 2 + (c + dc) % 2,
        )

    started = []

    def send(src, dst, sem, to):
        copy = pltpu.make_async_remote_copy(
            src_ref=src,
            dst_ref=dst,
            send_sem=send_sem.at[len(started)],
            recv_sem=sem,
            device_id=to,
            device_id_type=MESH,
        )
        copy.start()
        started.append(copy)

    def arrived(dst, sem):
        pltpu.make_async_remote_copy(
            src_ref=dst,
            dst_ref=dst,
            send_sem=send_sem.at[0],
            recv_sem=sem,
            device_id=device(dc=1),
            device_id_type=MESH,
        ).wait_recv()

    def q_at(slot):
        return qbuf.at[pl.ds(slot * CH, CH), :]

    def k_at(slot):
        return kbuf.at[pl.ds(slot * CH, CH), :]

    rows_copy = pltpu.make_async_copy(rows_hbm, rows, local_sem.at[0])
    rows_copy.start()
    codes_copy = pltpu.make_async_copy(codes_hbm, codes, local_sem.at[1])
    codes_copy.start()
    barrier = pltpu.get_barrier_semaphore()
    line = [(dx, dy) for dx in range(4) for dy in range(4) if (dx, dy) != (0, 0)]
    column = [(dz, dc) for dz in range(4) for dc in range(2) if (dz, dc) != (0, 0)]
    for dx, dy in line:
        pl.semaphore_signal(barrier, inc=1, device_id=device(dx=dx, dy=dy), device_id_type=MESH)
    for dz, dc in column:
        pl.semaphore_signal(barrier, inc=1, device_id=device(dz=dz, dc=dc), device_id_type=MESH)

    n_rows = rows.shape[0]
    ids = ids_ref[...]
    target = (ids // 2 - y + 4) % 4
    groups = lax.broadcasted_iota(jnp.int32, (16, n_rows), 0)
    onehot = jnp.where(groups == target, 1.0, 0.0)
    before = lax.broadcasted_iota(jnp.int32, (n_rows, n_rows), 0) < lax.broadcasted_iota(
        jnp.int32, (n_rows, n_rows), 1
    )
    earlier = jnp.dot(
        onehot.astype(jnp.bfloat16),
        jnp.where(before, 1.0, 0.0).astype(jnp.bfloat16),
        preferred_element_type=jnp.float32,
    )
    position = jnp.sum(
        onehot * (earlier + (groups * CH).astype(jnp.float32)), axis=0, keepdims=True
    ).astype(jnp.int32)
    slots = lax.broadcasted_iota(jnp.int32, (4 * CH, n_rows), 0)
    perm[...] = jnp.where(slots == position, 1.0, 0.0).astype(jnp.bfloat16)

    order = order_ref[...]
    pieces = []
    for cluster in range(2):
        own = jnp.where(ids % 2 == cluster, order, 0)
        pieces += [(own >> (8 * p)) & 255 for p in range(4)]
    pieces = jnp.concatenate(pieces + pieces, axis=0).astype(jnp.float32).astype(jnp.bfloat16)
    moved = lax.dot_general(
        pieces, perm[...], (((1,), (1,)), ((), ())), preferred_element_type=jnp.float32
    ).astype(jnp.int32)
    for d in range(4):
        for cluster in range(2):
            part = moved[4 * cluster : 4 * cluster + 4, d * CH : (d + 1) * CH]
            joined = part[0:1] + part[1:2] * 256 + part[2:3] * 65536 + part[3:4] * 16777216
            if d == 0:
                qord[0, cluster : cluster + 1, :] = joined
            else:
                sendo[d, cluster : cluster + 1, :] = joined
    for j in range(4):
        place = shard * 256 + (j % 2) * CH + lax.broadcasted_iota(jnp.int32, (1, CH), 1)
        live = place < counts_ref[j // 2]
        kord[0, j : j + 1, :] = jnp.where(live, key_order_ref[j : j + 1, :], DEAD)

    rows_copy.wait()
    values = rows[...].astype(jnp.float32)
    queries = (
        values * lax.rsqrt(jnp.sum(values * values, axis=-1, keepdims=True) + epsilon)
    ).astype(jnp.bfloat16)

    def picked(d):
        return jnp.dot(
            perm[pl.ds(d * CH, CH), :], queries, preferred_element_type=jnp.float32
        ).astype(jnp.bfloat16)

    qbuf[pl.ds(0, CH), :] = picked(0)
    for d in range(1, 4):
        sendq[d] = picked(d)

    pl.semaphore_wait(barrier, len(line) + len(column))

    def send_x(dy):
        here = q_at(Q_SLOT[0, dy])
        for dx, there in ((1, 3), (3, 1)):
            slot = Q_SLOT[there, dy]
            send(here, q_at(slot), q_sem.at[slot], device(dx=dx))

    send_x(0)
    for d in (1, 3, 2):
        slot = Q_SLOT[0, (4 - d) % 4]
        send(sendq.at[d], q_at(slot), q_sem.at[slot], device(dy=d))

    codes_copy.wait()

    def spread(slot_of, j):
        here = k_at(slot_of(0, 0, j))
        for to, place in (
            (device(dz=1), (3, 0, j)),
            (device(dz=3), (1, 0, j)),
            (device(dc=1), (0, 1, j)),
        ):
            send(here, k_at(K_SLOT[place]), k_sem.at[K_SLOT[place]], to)

    for j in J_ORDER:
        decoded = (
            codes[pl.ds(j * CH, CH), :].astype(jnp.float32) * scales_ref[j // 2 : j // 2 + 1, :]
            + offsets_ref[j // 2 : j // 2 + 1, :]
        )
        kbuf[pl.ds(K_SLOT[0, 0, j] * CH, CH), :] = (
            decoded * lax.rsqrt(jnp.sum(decoded * decoded, axis=-1, keepdims=True) + epsilon)
        ).astype(jnp.bfloat16)
        spread(lambda *place: K_SLOT[place], j)

    for dz, dc in column:
        slot = dc * 4 + (4 - dz) % 4
        send(kord.at[0], kord.at[slot], o_sem.at[0], device(dz=dz, dc=dc))
    for dx, dy in line:
        slot = Q_SLOT[(4 - dx) % 4, (4 - dy) % 4]
        source = sendo.at[dy] if dy else qord.at[0]
        send(source, qord.at[slot], o_sem.at[1], device(dx=dx, dy=dy))

    acc[...] = jnp.zeros_like(acc)
    arrived(kord.at[pl.ds(1, 7)], o_sem.at[0])
    for slot, (dz, dc, j) in enumerate(K_ORDER):
        row = kord[dc * 4 + dz, j : j + 1, :]
        kob[pl.ds(slot * CH, CH), :] = jnp.broadcast_to(row, (CH, CH)).T
    arrived(qord.at[pl.ds(1, 15)], o_sem.at[1])

    def tile(kt, qt):
        keys = kbuf[pl.ds(pl.multiple_of(kt * 4 * CH, 4 * CH), 4 * CH), :]
        asks = qbuf[pl.ds(pl.multiple_of(qt * 2 * CH, 2 * CH), 2 * CH), :]
        return lax.dot_general(
            keys, asks, (((1,), (1,)), ((), ())), preferred_element_type=jnp.float32
        )

    def keep(kt, qt, scores):
        key_order = kob[pl.ds(pl.multiple_of(kt * 4 * CH, 4 * CH), 4 * CH), :]
        cluster = kt % 2
        for h in range(2):
            limit = qord[qt * 2 + h, pl.ds(cluster, 1), :]
            part = jnp.where(key_order < limit, scores[:, h * CH : (h + 1) * CH], 0.0)
            best = jnp.max(part.reshape(4 * CH // 8, 8, CH), axis=0)
            acc[qt * 2 + h] = jnp.maximum(acc[qt * 2 + h], best)

    def work(count, place):
        def pair(i, carry):
            first, second = place(2 * i), place(2 * i + 1)
            s0, s1 = tile(*first), tile(*second)
            keep(*first, s0)
            keep(*second, s1)
            return carry

        lax.fori_loop(0, count // 2, pair, 0)
        if count % 2:
            last = place(count - 1)
            keep(*last, tile(*last))

    def other_core(place):
        dz, _, j = place
        slot = K_SLOT[dz, 1, j]
        send(k_at(K_SLOT[place]), k_at(slot), k_sem.at[slot], device(dc=1))

    def got_keys(*places):
        for place in places:
            arrived(k_at(K_SLOT[place]), k_sem.at[K_SLOT[place]])

    def got_queries(*places):
        for place in places:
            arrived(q_at(Q_SLOT[place]), q_sem.at[Q_SLOT[place]])

    for tick in range(1, 7):
        if tick <= 4:
            j, dy = J_ORDER[tick - 1], DY_ORDER[tick - 1]
            for ready in {1: (3,), 2: (1, 2)}.get(tick, ()):
                got_queries((0, ready))
                send_x(ready)
            got_keys((3, 0, j), (1, 0, j))
            if j % 2 == 0:
                slot = K_SLOT[2, 0, j]
                send(k_at(K_SLOT[3, 0, j]), k_at(slot), k_sem.at[slot], device(dz=1))
            else:
                slot = K_SLOT[2, 0, j]
                send(k_at(K_SLOT[1, 0, j]), k_at(slot), k_sem.at[slot], device(dz=3))
            other_core((3, 0, j))
            other_core((1, 0, j))
            got_queries((3, dy), (1, dy))
            slot = Q_SLOT[2, dy]
            if dy in (0, 1):
                send(q_at(Q_SLOT[3, dy]), q_at(slot), q_sem.at[slot], device(dx=1))
            else:
                send(q_at(Q_SLOT[1, dy]), q_at(slot), q_sem.at[slot], device(dx=3))
            if tick == 1:
                got_keys(*((0, 1, own) for own in J_ORDER))
            got_keys((3, 1, j), (1, 1, j))
        else:
            j = 2 * (tick - 5)
            got_keys((2, 0, j), (2, 0, j + 1))
            other_core((2, 0, j))
            other_core((2, 0, j + 1))
            got_queries(*Q_ORDER[2 * tick + 2 : 2 * tick + 4])
            got_keys((2, 1, j), (2, 1, j + 1))
        if tick == 1:
            work(6, lambda i: (i % 3, i // 3))
        elif tick == 2:
            def place(i):
                late = i // 8
                return (i % 4) * (1 - late) + 3 * late, (2 + i // 4) * (1 - late) + (i - 8) * late

            work(10, place)
        else:

            def place(i, n=tick + 2):
                late = i // n
                return i * (1 - late) + (n - 1) * late, (n - 1) * (1 - late) + (i - n) * late

            work(2 * tick + 3, place)

    for dx, dy in line:
        slot = Q_SLOT[(4 - dx) % 4, (4 - dy) % 4]
        send(acc.at[Q_SLOT[dx, dy]], ans.at[slot], o_sem.at[2], device(dx=dx, dy=dy))
    arrived(ans.at[pl.ds(1, 15)], o_sem.at[2])
    answers = []
    for d in range(4):
        best = acc[0] if d == 0 else ans[Q_SLOT[0, d]]
        for dx in range(1, 4):
            best = jnp.maximum(best, ans[Q_SLOT[dx, d]])
        answers.append(jnp.max(best, axis=0, keepdims=True))
    answer = jnp.concatenate(answers, axis=1)
    high = answer.astype(jnp.bfloat16).astype(jnp.float32)
    middle = (answer - high).astype(jnp.bfloat16).astype(jnp.float32)
    low = answer - high - middle
    parts = jnp.concatenate([high, middle, low, jnp.zeros((13, 4 * CH), jnp.float32)], axis=0)
    back = jnp.dot(parts.astype(jnp.bfloat16), perm[...], preferred_element_type=jnp.float32)
    out_ref[...] = back[0:1] + back[1:2] + back[2:3]
    for copy in started:
        copy.wait_send()


def per_device(new_rows, cluster_ids, new_order, codes, scales, offsets, counts, earlier_order):
    n_rows, width = new_rows.shape
    vmem = pl.BlockSpec(memory_space=pltpu.VMEM)
    anywhere = pl.BlockSpec(memory_space=pl.ANY)
    smem = pl.BlockSpec(memory_space=pltpu.SMEM)
    n_q, n_k = len(Q_ORDER), len(K_ORDER)
    out = pl.pallas_call(
        kernel,
        out_shape=jax.ShapeDtypeStruct((1, n_rows), jnp.float32),
        in_specs=[anywhere, vmem, vmem, anywhere, vmem, vmem, smem, vmem],
        out_specs=vmem,
        scratch_shapes=[
            pltpu.VMEM((n_rows, width), jnp.bfloat16),
            pltpu.VMEM((4 * CH, width), jnp.bfloat16),
            pltpu.VMEM((4, CH, width), jnp.bfloat16),
            pltpu.VMEM((4, 2, CH), jnp.int32),
            pltpu.VMEM((n_q * CH, width), jnp.bfloat16),
            pltpu.VMEM((n_k * CH, width), jnp.bfloat16),
            pltpu.VMEM((n_q, 2, CH), jnp.int32),
            pltpu.VMEM((8, 4, CH), jnp.int32),
            pltpu.VMEM((n_k * CH, CH), jnp.int32),
            pltpu.VMEM((n_q, 8, CH), jnp.float32),
            pltpu.VMEM((n_q, 8, CH), jnp.float32),
            pltpu.VMEM((4 * CH, n_rows), jnp.bfloat16),
            pltpu.SemaphoreType.DMA((2,)),
            pltpu.SemaphoreType.DMA((96,)),
            pltpu.SemaphoreType.DMA((n_q,)),
            pltpu.SemaphoreType.DMA((n_k,)),
            pltpu.SemaphoreType.DMA((3,)),
        ],
        compiler_params=pltpu.CompilerParams(
            collective_id=0, has_side_effects=True, vmem_limit_bytes=48 * 2**20
        ),
        cost_estimate=pl.CostEstimate(
            flops=2 * n_q * n_k * CH * CH * width, bytes_accessed=2**21, transcendentals=1024
        ),
    )(
        new_rows,
        cluster_ids.reshape(1, n_rows),
        new_order.reshape(1, n_rows),
        codes.reshape(4 * CH, width),
        scales,
        offsets,
        counts,
        earlier_order.reshape(4, CH),
    )
    return out.reshape(n_rows)


def solution(mesh):
    return jax.shard_map(
        per_device,
        mesh=mesh,
        in_specs=(
            P(("grp", "shard"), None),
            P(("grp", "shard")),
            P(("grp", "shard")),
            P("grp", "shard", None),
            P("grp", None),
            P("grp", None),
            P("grp"),
            P("grp", "shard"),
        ),
        out_specs=P(("grp", "shard")),
        check_vma=False,
    )
```

```python
import functools

import jax
import jax.numpy as jnp
from jax import lax
from jax.experimental import pallas as pl
from jax.experimental.pallas import tpu as pltpu
from jax.sharding import PartitionSpec as P

MESH = pl.DeviceIdType.MESH
epsilon = 1e-06
DEAD = 2147483647
CH = 128

Q_ORDER = [
    (0, 0), (0, 3),
    (3, 0), (1, 0),
    (0, 1), (0, 2),
    (3, 3), (1, 3),
    (3, 1), (1, 1),
    (3, 2), (1, 2),
    (2, 0), (2, 3),
    (2, 1), (2, 2),
]
Q_SLOT = {place: i for i, place in enumerate(Q_ORDER)}
K_ORDER = [
    (0, 0, 0), (0, 0, 1), (0, 1, 0), (0, 1, 1),
    (0, 0, 2), (0, 0, 3), (0, 1, 2), (0, 1, 3),
]
J_ORDER = [0, 2, 1, 3]
for _j in J_ORDER:
    K_ORDER += [(3, 0, _j), (3, 1, _j), (1, 0, _j), (1, 1, _j)]
for _j in (0, 2):
    K_ORDER += [(2, 0, _j), (2, 1, _j), (2, 0, _j + 1), (2, 1, _j + 1)]
K_SLOT = {place: i for i, place in enumerate(K_ORDER)}
DY_ORDER = [0, 3, 1, 2]


def kernel(
    rows_hbm, ids_hbm, order_hbm, codes_hbm, scales_hbm, offsets_hbm, counts_hbm, key_order_hbm,
    out_ref,
    rows, ids_ref, order_ref, codes, scales_ref, offsets_ref, counts_ref, key_order_ref,
    sendq, sendo, qbuf, kbuf, qord, kord, kob, acc, ans, perm,
    local_sem, send_sem, q_sem, k_sem, o_sem,
):
    y = lax.axis_index("grp")
    shard = lax.axis_index("shard")
    x, z, c = shard // 8, (shard // 2) % 4, shard % 2

    def device(dx=0, dy=0, dz=0, dc=0):
        return (
            (y + dy) % 4,
            (((x + dx) % 4) * 4 + (z + dz) % 4) * 2 + (c + dc) % 2,
        )

    started = []

    def send(src, dst, sem, to):
        copy = pltpu.make_async_remote_copy(
            src_ref=src,
            dst_ref=dst,
            send_sem=send_sem.at[len(started)],
            recv_sem=sem,
            device_id=to,
            device_id_type=MESH,
        )
        copy.start()
        started.append(copy)

    def arrived(dst, sem):
        pltpu.make_async_remote_copy(
            src_ref=dst,
            dst_ref=dst,
            send_sem=send_sem.at[0],
            recv_sem=sem,
            device_id=device(dc=1),
            device_id_type=MESH,
        ).wait_recv()

    def q_at(slot):
        return qbuf.at[pl.ds(slot * CH, CH), :]

    def k_at(slot):
        return kbuf.at[pl.ds(slot * CH, CH), :]

    loads = [
        pltpu.make_async_copy(src, dst, local_sem.at[i])
        for i, (src, dst) in enumerate(
            (
                (ids_hbm, ids_ref),
                (order_hbm, order_ref),
                (counts_hbm, counts_ref),
                (key_order_hbm, key_order_ref),
                (rows_hbm, rows),
                (scales_hbm, scales_ref),
                (offsets_hbm, offsets_ref),
                (codes_hbm, codes),
            )
        )
    ]
    for load in loads:
        load.start()
    barrier = pltpu.get_barrier_semaphore()
    line = [(dx, dy) for dx in range(4) for dy in range(4) if (dx, dy) != (0, 0)]
    column = [(dz, dc) for dz in range(4) for dc in range(2) if (dz, dc) != (0, 0)]
    for dx, dy in line:
        pl.semaphore_signal(barrier, inc=1, device_id=device(dx=dx, dy=dy), device_id_type=MESH)
    for dz, dc in column:
        pl.semaphore_signal(barrier, inc=1, device_id=device(dz=dz, dc=dc), device_id_type=MESH)

    n_rows = rows.shape[0]
    for load in loads[:4]:
        load.wait()
    ids = ids_ref[...]
    target = (ids // 2 - y + 4) % 4
    groups = lax.broadcasted_iota(jnp.int32, (16, n_rows), 0)
    onehot = jnp.where(groups == target, 1.0, 0.0)
    before = lax.broadcasted_iota(jnp.int32, (n_rows, n_rows), 0) < lax.broadcasted_iota(
        jnp.int32, (n_rows, n_rows), 1
    )
    earlier = jnp.dot(
        onehot.astype(jnp.bfloat16),
        jnp.where(before, 1.0, 0.0).astype(jnp.bfloat16),
        preferred_element_type=jnp.float32,
    )
    position = jnp.sum(
        onehot * (earlier + (groups * CH).astype(jnp.float32)), axis=0, keepdims=True
    ).astype(jnp.int32)
    slots = lax.broadcasted_iota(jnp.int32, (4 * CH, n_rows), 0)
    perm[...] = jnp.where(slots == position, 1.0, 0.0).astype(jnp.bfloat16)

    order = order_ref[...]
    pieces = []
    for cluster in range(2):
        own = jnp.where(ids % 2 == cluster, order, 0)
        pieces += [(own >> (8 * p)) & 255 for p in range(4)]
    pieces = jnp.concatenate(pieces + pieces, axis=0).astype(jnp.float32).astype(jnp.bfloat16)
    moved = lax.dot_general(
        pieces, perm[...], (((1,), (1,)), ((), ())), preferred_element_type=jnp.float32
    ).astype(jnp.int32)
    for d in range(4):
        for cluster in range(2):
            part = moved[4 * cluster : 4 * cluster + 4, d * CH : (d + 1) * CH]
            joined = part[0:1] + part[1:2] * 256 + part[2:3] * 65536 + part[3:4] * 16777216
            if d == 0:
                qord[0, cluster : cluster + 1, :] = joined
            else:
                sendo[d, cluster : cluster + 1, :] = joined
    for j in range(4):
        place = shard * 256 + (j % 2) * CH + lax.broadcasted_iota(jnp.int32, (1, CH), 1)
        live = place < counts_ref[j // 2]
        kord[0, j : j + 1, :] = jnp.where(
            live, key_order_ref[j // 2 : j // 2 + 1, (j % 2) * CH : (j % 2 + 1) * CH], DEAD
        )

    loads[4].wait()
    values = rows[...].astype(jnp.float32)
    queries = (
        values * lax.rsqrt(jnp.sum(values * values, axis=-1, keepdims=True) + epsilon)
    ).astype(jnp.bfloat16)

    def picked(d):
        return jnp.dot(
            perm[pl.ds(d * CH, CH), :], queries, preferred_element_type=jnp.float32
        ).astype(jnp.bfloat16)

    qbuf[pl.ds(0, CH), :] = picked(0)
    for d in range(1, 4):
        sendq[d] = picked(d)

    pl.semaphore_wait(barrier, len(line) + len(column))

    def send_x(dy):
        here = q_at(Q_SLOT[0, dy])
        for dx, there in ((1, 3), (3, 1)):
            slot = Q_SLOT[there, dy]
            send(here, q_at(slot), q_sem.at[slot], device(dx=dx))

    for dz, dc in column:
        slot = dc * 4 + (4 - dz) % 4
        send(kord.at[0], kord.at[slot], o_sem.at[0], device(dz=dz, dc=dc))
    for dx, dy in line:
        slot = Q_SLOT[(4 - dx) % 4, (4 - dy) % 4]
        source = sendo.at[dy] if dy else qord.at[0]
        send(source, qord.at[slot], o_sem.at[1], device(dx=dx, dy=dy))

    send_x(0)
    for d in (1, 3, 2):
        slot = Q_SLOT[0, (4 - d) % 4]
        send(sendq.at[d], q_at(slot), q_sem.at[slot], device(dy=d))

    for load in loads[5:]:
        load.wait()

    def spread(slot_of, j):
        here = k_at(slot_of(0, 0, j))
        for to, place in (
            (device(dz=1), (3, 0, j)),
            (device(dz=3), (1, 0, j)),
            (device(dc=1), (0, 1, j)),
        ):
            send(here, k_at(K_SLOT[place]), k_sem.at[K_SLOT[place]], to)

    for j in J_ORDER:
        decoded = (
            codes[pl.ds(j * CH, CH), :].astype(jnp.float32) * scales_ref[j // 2 : j // 2 + 1, :]
            + offsets_ref[j // 2 : j // 2 + 1, :]
        )
        kbuf[pl.ds(K_SLOT[0, 0, j] * CH, CH), :] = (
            decoded * lax.rsqrt(jnp.sum(decoded * decoded, axis=-1, keepdims=True) + epsilon)
        ).astype(jnp.bfloat16)
        spread(lambda *place: K_SLOT[place], j)

    acc[...] = jnp.zeros_like(acc)
    arrived(kord.at[pl.ds(1, 7)], o_sem.at[0])
    for slot, (dz, dc, j) in enumerate(K_ORDER):
        row = kord[dc * 4 + dz, j : j + 1, :]
        kob[pl.ds(slot * CH, CH), :] = jnp.broadcast_to(row, (CH, CH)).T
    arrived(qord.at[pl.ds(1, 15)], o_sem.at[1])

    def tile(key_row, n_keys, block, n_blocks):
        keys = kbuf[pl.ds(pl.multiple_of(key_row, 2 * CH), n_keys), :]
        asks = qbuf[pl.ds(pl.multiple_of(block * CH, CH), n_blocks * CH), :]
        return lax.dot_general(
            keys, asks, (((1,), (1,)), ((), ())), preferred_element_type=jnp.float32
        )

    def keep(key_row, n_keys, block, n_blocks, scores):
        key_order = kob[pl.ds(pl.multiple_of(key_row, 2 * CH), n_keys), :]
        cluster = (key_row // (4 * CH)) % 2
        for h in range(n_blocks):
            limit = qord[block + h, pl.ds(cluster, 1), :]
            part = jnp.where(key_order < limit, scores[:, h * CH : (h + 1) * CH], 0.0)
            best = jnp.max(part.reshape(n_keys // 8, 8, CH), axis=0)
            acc[block + h] = jnp.maximum(acc[block + h], best)

    def work(count, place, n_keys, n_blocks, together):
        def some(first, size):
            at = [place(first + i) for i in range(size)]
            scores = [tile(row, n_keys, block, n_blocks) for row, block in at]
            for (row, block), found in zip(at, scores):
                keep(row, n_keys, block, n_blocks, found)

        def step(i, carry):
            some(together * i, together)
            return carry

        lax.fori_loop(0, count // together, step, 0)
        if count % together:
            some(count - count % together, count % together)

    def new_queries(qt, n_qt, n_kt):
        work(
            n_kt * n_qt, lambda i: ((i % n_kt) * 4 * CH, (qt + i // n_kt) * 2), 4 * CH, 2, 2
        )

    def new_keys(kt, n_qt):
        work(n_qt // 2, lambda i: (kt * 4 * CH, i * 4), 4 * CH, 4, 1)
        if n_qt % 2:
            work(1, lambda i: (kt * 4 * CH, (n_qt - 1) * 2), 4 * CH, 2, 1)

    def other_core(place):
        dz, _, j = place
        slot = K_SLOT[dz, 1, j]
        send(k_at(K_SLOT[place]), k_at(slot), k_sem.at[slot], device(dc=1))

    def got_keys(*places):
        for place in places:
            arrived(k_at(K_SLOT[place]), k_sem.at[K_SLOT[place]])

    def got_queries(*places):
        for place in places:
            arrived(q_at(Q_SLOT[place]), q_sem.at[Q_SLOT[place]])

    for tick in range(1, 7):
        if tick <= 4:
            j, dy = J_ORDER[tick - 1], DY_ORDER[tick - 1]
            for ready in {1: (3,), 2: (1, 2)}.get(tick, ()):
                got_queries((0, ready))
                send_x(ready)
            got_keys((3, 0, j), (1, 0, j))
            slot = K_SLOT[2, 0, j]
            if j % 2 == 0:
                send(k_at(K_SLOT[3, 0, j]), k_at(slot), k_sem.at[slot], device(dz=1))
            else:
                send(k_at(K_SLOT[1, 0, j]), k_at(slot), k_sem.at[slot], device(dz=3))
            other_core((3, 0, j))
            other_core((1, 0, j))
            got_queries((3, dy), (1, dy))
            slot = Q_SLOT[2, dy]
            if dy in (0, 1):
                send(q_at(Q_SLOT[3, dy]), q_at(slot), q_sem.at[slot], device(dx=1))
            else:
                send(q_at(Q_SLOT[1, dy]), q_at(slot), q_sem.at[slot], device(dx=3))
            if tick == 1:
                got_keys(*((0, 1, own) for own in J_ORDER))
                new_queries(0, 2, 2)
                n_q = 2
            elif tick == 2:
                new_queries(2, 2, 3)
                n_q = 4
            else:
                new_queries(tick + 1, 1, tick + 1)
                n_q = tick + 2
            got_keys((3, 1, j), (1, 1, j))
            new_keys(tick + 1, n_q)
        else:
            j = 2 * (tick - 5)
            got_queries(*Q_ORDER[2 * tick + 2 : 2 * tick + 4])
            if tick == 6:
                new_queries(7, 1, 7)
            got_keys((2, 0, j), (2, 0, j + 1))
            other_core((2, 0, j))
            other_core((2, 0, j + 1))
            if tick == 5:
                new_queries(6, 1, 6)
            got_keys((2, 1, j), (2, 1, j + 1))
            new_keys(tick + 1, tick + 2)

    for dx, dy in line:
        slot = Q_SLOT[(4 - dx) % 4, (4 - dy) % 4]
        send(acc.at[Q_SLOT[dx, dy]], ans.at[slot], o_sem.at[2], device(dx=dx, dy=dy))
    arrived(ans.at[pl.ds(1, 15)], o_sem.at[2])
    answers = []
    for d in range(4):
        best = acc[0] if d == 0 else ans[Q_SLOT[0, d]]
        for dx in range(1, 4):
            best = jnp.maximum(best, ans[Q_SLOT[dx, d]])
        answers.append(jnp.max(best, axis=0, keepdims=True))
    answer = jnp.concatenate(answers, axis=1)
    high = answer.astype(jnp.bfloat16).astype(jnp.float32)
    middle = (answer - high).astype(jnp.bfloat16).astype(jnp.float32)
    low = answer - high - middle
    parts = jnp.concatenate([high, middle, low, jnp.zeros((13, 4 * CH), jnp.float32)], axis=0)
    back = jnp.dot(parts.astype(jnp.bfloat16), perm[...], preferred_element_type=jnp.float32)
    out_ref[...] = back[0:1] + back[1:2] + back[2:3]
    for copy in started:
        copy.wait_send()


def per_device(new_rows, cluster_ids, new_order, codes, scales, offsets, counts, earlier_order):
    n_rows, width = new_rows.shape
    vmem = pl.BlockSpec(memory_space=pltpu.VMEM)
    n_q, n_k = len(Q_ORDER), len(K_ORDER)
    out = pl.pallas_call(
        kernel,
        out_shape=jax.ShapeDtypeStruct((1, n_rows), jnp.float32),
        in_specs=[pl.BlockSpec(memory_space=pl.ANY)] * 8,
        out_specs=vmem,
        scratch_shapes=[
            pltpu.VMEM((n_rows, width), jnp.bfloat16),
            pltpu.VMEM((1, n_rows), jnp.int32),
            pltpu.VMEM((1, n_rows), jnp.int32),
            pltpu.VMEM((4 * CH, width), jnp.bfloat16),
            pltpu.VMEM((2, width), jnp.float32),
            pltpu.VMEM((2, width), jnp.float32),
            pltpu.SMEM((2,), jnp.int32),
            pltpu.VMEM((2, 2 * CH), jnp.int32),
            pltpu.VMEM((4, CH, width), jnp.bfloat16),
            pltpu.VMEM((4, 2, CH), jnp.int32),
            pltpu.VMEM((n_q * CH, width), jnp.bfloat16),
            pltpu.VMEM((n_k * CH, width), jnp.bfloat16),
            pltpu.VMEM((n_q, 2, CH), jnp.int32),
            pltpu.VMEM((8, 4, CH), jnp.int32),
            pltpu.VMEM((n_k * CH, CH), jnp.int32),
            pltpu.VMEM((n_q, 8, CH), jnp.float32),
            pltpu.VMEM((n_q, 8, CH), jnp.float32),
            pltpu.VMEM((4 * CH, n_rows), jnp.bfloat16),
            pltpu.SemaphoreType.DMA((8,)),
            pltpu.SemaphoreType.DMA((96,)),
            pltpu.SemaphoreType.DMA((n_q,)),
            pltpu.SemaphoreType.DMA((n_k,)),
            pltpu.SemaphoreType.DMA((3,)),
        ],
        compiler_params=pltpu.CompilerParams(
            collective_id=0, has_side_effects=True, vmem_limit_bytes=63 * 2**20
        ),
        cost_estimate=pl.CostEstimate(
            flops=2 * n_q * n_k * CH * CH * width, bytes_accessed=2**21, transcendentals=1024
        ),
    )(
        new_rows,
        cluster_ids.reshape(1, n_rows),
        new_order.reshape(1, n_rows),
        codes.reshape(4 * CH, width),
        scales,
        offsets,
        counts,
        earlier_order,
    )
    return out.reshape(n_rows)


def solution(mesh):
    return jax.shard_map(
        per_device,
        mesh=mesh,
        in_specs=(
            P(("grp", "shard"), None),
            P(("grp", "shard")),
            P(("grp", "shard")),
            P("grp", "shard", None),
            P("grp", None),
            P("grp", None),
            P("grp"),
            P("grp", "shard"),
        ),
        out_specs=P(("grp", "shard")),
        check_vma=False,
    )
```

```python
import functools

import jax
import jax.numpy as jnp
from jax import lax
from jax.experimental import pallas as pl
from jax.experimental.pallas import tpu as pltpu
from jax.sharding import PartitionSpec as P

MESH = pl.DeviceIdType.MESH
epsilon = 1e-06
DEAD = 2147483647
CH = 128
HALF = CH // 2

Q_ORDER = [
    (0, 0), (0, 3),
    (3, 0), (1, 0),
    (0, 1), (0, 2),
    (3, 3), (1, 3),
    (3, 1), (1, 1),
    (3, 2), (1, 2),
    (2, 0), (2, 3),
    (2, 1), (2, 2),
]
Q_SLOT = {place: i for i, place in enumerate(Q_ORDER)}
K_ORDER = [
    (0, 0, 0), (0, 0, 1), (0, 1, 0), (0, 1, 1),
    (0, 0, 2), (0, 0, 3), (0, 1, 2), (0, 1, 3),
]
J_ORDER = [0, 2, 1, 3]
for _j in J_ORDER:
    K_ORDER += [(3, 0, _j), (3, 1, _j), (1, 0, _j), (1, 1, _j)]
for _j in (0, 2):
    K_ORDER += [(2, 0, _j), (2, 1, _j), (2, 0, _j + 1), (2, 1, _j + 1)]
K_ROW = {
    place + (h,): i * CH + h * HALF if i < 28 else 28 * CH + h * 4 * HALF + (i - 28) * HALF
    for i, place in enumerate(K_ORDER)
    for h in range(2)
}
DY_ORDER = [0, 3, 1, 2]


def kernel(
    rows_hbm, ids_hbm, order_hbm, codes_hbm, scales_hbm, offsets_hbm, counts_hbm, key_order_hbm,
    out_ref,
    rows, ids_ref, order_ref, codes, scales_ref, offsets_ref, counts_ref, key_order_ref,
    sendq, sendo, qbuf, kbuf, qord, kord, kob, acc, ans, perm,
    local_sem, send_sem, q_sem, k_sem, o_sem,
):
    y = lax.axis_index("grp")
    shard = lax.axis_index("shard")
    x, z, c = shard // 8, (shard // 2) % 4, shard % 2

    def device(dx=0, dy=0, dz=0, dc=0):
        return (
            (y + dy) % 4,
            (((x + dx) % 4) * 4 + (z + dz) % 4) * 2 + (c + dc) % 2,
        )

    started = []

    def send(src, dst, sem, to):
        copy = pltpu.make_async_remote_copy(
            src_ref=src,
            dst_ref=dst,
            send_sem=send_sem.at[len(started)],
            recv_sem=sem,
            device_id=to,
            device_id_type=MESH,
        )
        copy.start()
        started.append(copy)

    def arrived(dst, sem):
        pltpu.make_async_remote_copy(
            src_ref=dst,
            dst_ref=dst,
            send_sem=send_sem.at[0],
            recv_sem=sem,
            device_id=device(dc=1),
            device_id_type=MESH,
        ).wait_recv()

    def q_half(place, h):
        slot = Q_SLOT[place]
        return qbuf.at[pl.ds(slot * CH + h * HALF, HALF), :], q_sem.at[2 * slot + h]

    def k_part(place, h=None):
        row = K_ROW[place + (h or 0,)]
        return kbuf.at[pl.ds(row, CH if h is None else HALF), :], k_sem.at[row // HALF]

    loads = [
        pltpu.make_async_copy(src, dst, local_sem.at[i])
        for i, (src, dst) in enumerate(
            (
                (ids_hbm, ids_ref),
                (order_hbm, order_ref),
                (counts_hbm, counts_ref),
                (key_order_hbm, key_order_ref),
                (rows_hbm, rows),
                (scales_hbm, scales_ref),
                (offsets_hbm, offsets_ref),
                (codes_hbm, codes),
            )
        )
    ]
    for load in loads:
        load.start()
    barrier = pltpu.get_barrier_semaphore()
    line = [(dx, dy) for dx in range(4) for dy in range(4) if (dx, dy) != (0, 0)]
    column = [(dz, dc) for dz in range(4) for dc in range(2) if (dz, dc) != (0, 0)]
    for dx, dy in line:
        pl.semaphore_signal(barrier, inc=1, device_id=device(dx=dx, dy=dy), device_id_type=MESH)
    for dz, dc in column:
        pl.semaphore_signal(barrier, inc=1, device_id=device(dz=dz, dc=dc), device_id_type=MESH)

    n_rows = rows.shape[0]
    for load in loads[:4]:
        load.wait()
    ids = ids_ref[...]
    target = (ids // 2 - y + 4) % 4
    groups = lax.broadcasted_iota(jnp.int32, (16, n_rows), 0)
    onehot = jnp.where(groups == target, 1.0, 0.0)
    before = lax.broadcasted_iota(jnp.int32, (n_rows, n_rows), 0) < lax.broadcasted_iota(
        jnp.int32, (n_rows, n_rows), 1
    )
    earlier = jnp.dot(
        onehot.astype(jnp.bfloat16),
        jnp.where(before, 1.0, 0.0).astype(jnp.bfloat16),
        preferred_element_type=jnp.float32,
    )
    position = jnp.sum(
        onehot * (earlier + (groups * CH).astype(jnp.float32)), axis=0, keepdims=True
    ).astype(jnp.int32)
    slots = lax.broadcasted_iota(jnp.int32, (4 * CH, n_rows), 0)
    perm[...] = jnp.where(slots == position, 1.0, 0.0).astype(jnp.bfloat16)

    order = order_ref[...]
    pieces = []
    for cluster in range(2):
        own = jnp.where(ids % 2 == cluster, order, 0)
        pieces += [(own >> (8 * p)) & 255 for p in range(4)]
    pieces = jnp.concatenate(pieces + pieces, axis=0).astype(jnp.float32).astype(jnp.bfloat16)
    moved = lax.dot_general(
        pieces, perm[...], (((1,), (1,)), ((), ())), preferred_element_type=jnp.float32
    ).astype(jnp.int32)
    for d in range(4):
        for cluster in range(2):
            part = moved[4 * cluster : 4 * cluster + 4, d * CH : (d + 1) * CH]
            joined = part[0:1] + part[1:2] * 256 + part[2:3] * 65536 + part[3:4] * 16777216
            if d == 0:
                qord[0, cluster : cluster + 1, :] = joined
            else:
                sendo[d, cluster : cluster + 1, :] = joined
    for j in range(4):
        place = shard * 256 + (j % 2) * CH + lax.broadcasted_iota(jnp.int32, (1, CH), 1)
        live = place < counts_ref[j // 2]
        kord[0, j : j + 1, :] = jnp.where(
            live, key_order_ref[j // 2 : j // 2 + 1, (j % 2) * CH : (j % 2 + 1) * CH], DEAD
        )

    loads[4].wait()
    values = rows[...].astype(jnp.float32)
    queries = (
        values * lax.rsqrt(jnp.sum(values * values, axis=-1, keepdims=True) + epsilon)
    ).astype(jnp.bfloat16)

    def picked(d):
        return jnp.dot(
            perm[pl.ds(d * CH, CH), :], queries, preferred_element_type=jnp.float32
        ).astype(jnp.bfloat16)

    qbuf[pl.ds(0, CH), :] = picked(0)
    for d in range(1, 4):
        sendq[d] = picked(d)

    pl.semaphore_wait(barrier, len(line) + len(column))

    def send_x(dy, h):
        here, _ = q_half((0, dy), h)
        for dx, there in ((1, 3), (3, 1)):
            send(here, *q_half((there, dy), h), device(dx=dx))

    def send_y(d, h):
        send(sendq.at[d, pl.ds(h * HALF, HALF)], *q_half((0, (4 - d) % 4), h), device(dy=d))

    for dz, dc in column:
        slot = dc * 4 + (4 - dz) % 4
        send(kord.at[0], kord.at[slot], o_sem.at[0], device(dz=dz, dc=dc))
    for dx, dy in line:
        slot = Q_SLOT[(4 - dx) % 4, (4 - dy) % 4]
        source = sendo.at[dy] if dy else qord.at[0]
        send(source, qord.at[slot], o_sem.at[1], device(dx=dx, dy=dy))

    for h in range(2):
        for d in (1, 3):
            send_y(d, h)
        send_x(0, h)

    for load in loads[5:]:
        load.wait()

    def spread(j):
        here, _ = k_part((0, 0, j))
        for to, place in (
            (device(dz=1), (3, 0, j)),
            (device(dz=3), (1, 0, j)),
            (device(dc=1), (0, 1, j)),
        ):
            send(here, *k_part(place), to)

    for j in J_ORDER:
        decoded = (
            codes[pl.ds(j * CH, CH), :].astype(jnp.float32) * scales_ref[j // 2 : j // 2 + 1, :]
            + offsets_ref[j // 2 : j // 2 + 1, :]
        )
        kbuf[pl.ds(K_ROW[0, 0, j, 0], CH), :] = (
            decoded * lax.rsqrt(jnp.sum(decoded * decoded, axis=-1, keepdims=True) + epsilon)
        ).astype(jnp.bfloat16)
        spread(j)

    acc[...] = jnp.zeros_like(acc)
    arrived(kord.at[pl.ds(1, 7)], o_sem.at[0])
    for dz, dc, j in K_ORDER:
        turned = jnp.broadcast_to(kord[dc * 4 + dz, j : j + 1, :], (CH, CH)).T
        for h in range(2):
            kob[pl.ds(K_ROW[dz, dc, j, h], HALF), :] = turned[h * HALF : (h + 1) * HALF]
    arrived(qord.at[pl.ds(1, 15)], o_sem.at[1])

    def tile(key_row, n_keys, block, n_blocks):
        keys = kbuf[pl.ds(pl.multiple_of(key_row, 2 * CH), n_keys), :]
        asks = qbuf[pl.ds(pl.multiple_of(block * CH, CH), n_blocks * CH), :]
        return lax.dot_general(
            keys, asks, (((1,), (1,)), ((), ())), preferred_element_type=jnp.float32
        )

    def keep(key_row, n_keys, block, n_blocks, scores):
        key_order = kob[pl.ds(pl.multiple_of(key_row, 2 * CH), n_keys), :]
        cluster = (key_row // (4 * CH)) % 2
        for h in range(n_blocks):
            limit = qord[block + h, pl.ds(cluster, 1), :]
            part = jnp.where(key_order < limit, scores[:, h * CH : (h + 1) * CH], 0.0)
            best = jnp.max(part.reshape(n_keys // 8, 8, CH), axis=0)
            acc[block + h] = jnp.maximum(acc[block + h], best)

    def tiles(*items):
        scores = [tile(*item) for item in items]
        for item, found in zip(items, scores):
            keep(*item, found)

    def work(count, place, n_keys, n_blocks, together):
        def some(first, size):
            at = [place(first + i) for i in range(size)]
            scores = [tile(row, n_keys, block, n_blocks) for row, block in at]
            for (row, block), found in zip(at, scores):
                keep(row, n_keys, block, n_blocks, found)

        def step(i, carry):
            some(together * i, together)
            return carry

        lax.fori_loop(0, count // together, step, 0)
        if count % together:
            some(count - count % together, count % together)

    def new_queries(qt, n_qt, n_kt):
        work(
            n_kt * n_qt, lambda i: ((i % n_kt) * 4 * CH, (qt + i // n_kt) * 2), 4 * CH, 2, 2
        )

    def new_keys(row, n_keys, n_qt):
        work(n_qt // 2, lambda i: (row, i * 4), n_keys, 4, 1)
        if n_qt % 2:
            work(1, lambda i: (row, (n_qt - 1) * 2), n_keys, 2, 1)

    def other_core(place, h=None):
        dz, _, j = place
        send(k_part(place, h)[0], *k_part((dz, 1, j), h), device(dc=1))

    def got_keys(*places, h=None):
        for place in places:
            arrived(*k_part(place, h))

    def got_queries(place, h):
        arrived(*q_half(place, h))

    for tick in range(1, 7):
        if tick <= 4:
            j, dy = J_ORDER[tick - 1], DY_ORDER[tick - 1]
            for ready in {1: (3, 1), 2: (2,)}.get(tick, ()):
                for h in range(2):
                    got_queries((0, ready), h)
                    send_x(ready, h)
            if tick == 1:
                for h in range(2):
                    send_y(2, h)
            got_keys((3, 0, j), (1, 0, j))
            side, to = ((3, 1), (1, 3))[j % 2]
            if j < 2:
                send(k_part((side, 0, j))[0], *k_part((2, 0, j)), device(dz=to))
            else:
                for h in range(2):
                    row = K_ROW[side, 0, j, h]
                    send(kbuf.at[pl.ds(row, HALF), :], *k_part((2, 0, j), h), device(dz=to))
            other_core((3, 0, j))
            other_core((1, 0, j))
            for h in range(2):
                got_queries((3, dy), h)
                got_queries((1, dy), h)
            for passed in {2: (0, 3), 3: (1,), 4: (2,)}.get(tick, ()):
                side, to = (3, 1) if passed in (0, 1) else (1, 3)
                for h in range(2):
                    send(
                        q_half((side, passed), h)[0], *q_half((2, passed), h), device(dx=to)
                    )
            if tick == 1:
                got_keys(*((0, 1, own) for own in J_ORDER))
                new_queries(0, 2, 2)
                n_q = 2
            elif tick == 2:
                new_queries(2, 2, 3)
                n_q = 4
            else:
                new_queries(tick + 1, 1, tick + 1)
                n_q = tick + 2
            got_keys((3, 1, j), (1, 1, j))
            new_keys((tick + 1) * 4 * CH, 4 * CH, n_q)
        elif tick == 5:
            got_keys((2, 0, 0), (2, 0, 1))
            other_core((2, 0, 0))
            other_core((2, 0, 1))
            for dy in (0, 3):
                for h in range(2):
                    got_queries((2, dy), h)
            tiles(*((kt * 4 * CH, 4 * CH, 12, 2) for kt in range(6)))
            got_keys((2, 1, 0), (2, 1, 1))
            tiles((6 * 4 * CH, 4 * CH, 0, 14))
        else:
            last = 7 * 4 * CH
            got_keys((2, 0, 2), (2, 0, 3), h=0)
            other_core((2, 0, 2), 0)
            other_core((2, 0, 3), 0)
            got_keys((2, 1, 2), (2, 1, 3), h=0)
            tiles((last, 2 * CH, 0, 14))
            for dy in (1, 2):
                for h in range(2):
                    got_queries((2, dy), h)
            tiles(*((kt * 4 * CH, 4 * CH, 14, 2) for kt in range(4)))
            got_keys((2, 0, 2), (2, 0, 3), h=1)
            other_core((2, 0, 2), 1)
            other_core((2, 0, 3), 1)
            tiles(
                *((kt * 4 * CH, 4 * CH, 14, 2) for kt in range(4, 7)), (last, 2 * CH, 14, 2)
            )
            got_keys((2, 1, 2), (2, 1, 3), h=1)
            tiles((last + 2 * CH, 2 * CH, 0, 16))

    for dx, dy in line:
        slot = Q_SLOT[(4 - dx) % 4, (4 - dy) % 4]
        send(acc.at[Q_SLOT[dx, dy]], ans.at[slot], o_sem.at[2], device(dx=dx, dy=dy))
    arrived(ans.at[pl.ds(1, 15)], o_sem.at[2])
    answers = []
    for d in range(4):
        best = acc[0] if d == 0 else ans[Q_SLOT[0, d]]
        for dx in range(1, 4):
            best = jnp.maximum(best, ans[Q_SLOT[dx, d]])
        answers.append(jnp.max(best, axis=0, keepdims=True))
    answer = jnp.concatenate(answers, axis=1)
    high = answer.astype(jnp.bfloat16).astype(jnp.float32)
    middle = (answer - high).astype(jnp.bfloat16).astype(jnp.float32)
    low = answer - high - middle
    parts = jnp.concatenate([high, middle, low, jnp.zeros((13, 4 * CH), jnp.float32)], axis=0)
    back = jnp.dot(parts.astype(jnp.bfloat16), perm[...], preferred_element_type=jnp.float32)
    out_ref[...] = back[0:8]
    for copy in started:
        copy.wait_send()


def per_device(new_rows, cluster_ids, new_order, codes, scales, offsets, counts, earlier_order):
    n_rows, width = new_rows.shape
    vmem = pl.BlockSpec(memory_space=pltpu.VMEM)
    n_q, n_k = len(Q_ORDER), len(K_ORDER)
    out = pl.pallas_call(
        kernel,
        out_shape=jax.ShapeDtypeStruct((8, n_rows), jnp.float32),
        in_specs=[pl.BlockSpec(memory_space=pl.ANY)] * 8,
        out_specs=vmem,
        scratch_shapes=[
            pltpu.VMEM((n_rows, width), jnp.bfloat16),
            pltpu.VMEM((1, n_rows), jnp.int32),
            pltpu.VMEM((1, n_rows), jnp.int32),
            pltpu.VMEM((4 * CH, width), jnp.bfloat16),
            pltpu.VMEM((2, width), jnp.float32),
            pltpu.VMEM((2, width), jnp.float32),
            pltpu.SMEM((2,), jnp.int32),
            pltpu.VMEM((2, 2 * CH), jnp.int32),
            pltpu.VMEM((4, CH, width), jnp.bfloat16),
            pltpu.VMEM((4, 2, CH), jnp.int32),
            pltpu.VMEM((n_q * CH, width), jnp.bfloat16),
            pltpu.VMEM((n_k * CH, width), jnp.bfloat16),
            pltpu.VMEM((n_q, 2, CH), jnp.int32),
            pltpu.VMEM((8, 4, CH), jnp.int32),
            pltpu.VMEM((n_k * CH, CH), jnp.int32),
            pltpu.VMEM((n_q, 8, CH), jnp.float32),
            pltpu.VMEM((n_q, 8, CH), jnp.float32),
            pltpu.VMEM((4 * CH, n_rows), jnp.bfloat16),
            pltpu.SemaphoreType.DMA((8,)),
            pltpu.SemaphoreType.DMA((128,)),
            pltpu.SemaphoreType.DMA((2 * n_q,)),
            pltpu.SemaphoreType.DMA((2 * n_k,)),
            pltpu.SemaphoreType.DMA((3,)),
        ],
        compiler_params=pltpu.CompilerParams(
            collective_id=0, has_side_effects=True, vmem_limit_bytes=63 * 2**20
        ),
        cost_estimate=pl.CostEstimate(
            flops=2 * n_q * n_k * CH * CH * width, bytes_accessed=2**21, transcendentals=1024
        ),
    )(
        new_rows,
        cluster_ids.reshape(1, n_rows),
        new_order.reshape(1, n_rows),
        codes.reshape(4 * CH, width),
        scales,
        offsets,
        counts,
        earlier_order,
    )
    return out[0] + out[1] + out[2]


def solution(mesh):
    return jax.shard_map(
        per_device,
        mesh=mesh,
        in_specs=(
            P(("grp", "shard"), None),
            P(("grp", "shard")),
            P(("grp", "shard")),
            P("grp", "shard", None),
            P("grp", None),
            P("grp", None),
            P("grp"),
            P("grp", "shard"),
        ),
        out_specs=P(("grp", "shard")),
        check_vma=False,
    )
```

```python
import functools

import jax
import jax.numpy as jnp
from jax import lax
from jax.experimental import pallas as pl
from jax.experimental.pallas import tpu as pltpu
from jax.sharding import PartitionSpec as P

MESH = pl.DeviceIdType.MESH
epsilon = 1e-06
DEAD = 2147483647
CH = 128
HALF = CH // 2

Q_ORDER = [
    (0, 0), (0, 3),
    (3, 0), (1, 0),
    (0, 1), (0, 2),
    (3, 3), (1, 3),
    (3, 1), (1, 1),
    (3, 2), (1, 2),
    (2, 0), (2, 3),
    (2, 1), (2, 2),
]
Q_SLOT = {place: i for i, place in enumerate(Q_ORDER)}
K_ORDER = [
    (0, 0, 0), (0, 0, 1), (0, 1, 0), (0, 1, 1),
    (0, 0, 2), (0, 0, 3), (0, 1, 2), (0, 1, 3),
]
J_ORDER = [0, 2, 1, 3]
for _j in J_ORDER:
    K_ORDER += [(3, 0, _j), (3, 1, _j), (1, 0, _j), (1, 1, _j)]
for _j in (0, 2):
    K_ORDER += [(2, 0, _j), (2, 1, _j), (2, 0, _j + 1), (2, 1, _j + 1)]
K_ROW = {
    place + (h,): i * CH + h * HALF if i < 28 else 28 * CH + h * 4 * HALF + (i - 28) * HALF
    for i, place in enumerate(K_ORDER)
    for h in range(2)
}
DY_ORDER = [0, 3, 1, 2]


def kernel(
    rows_hbm, ids_hbm, order_hbm, codes_hbm, scales_hbm, offsets_hbm, counts_hbm, key_order_hbm,
    out_ref,
    rows, ids_ref, order_ref, codes, scales_ref, offsets_ref, counts_ref, key_order_ref,
    sendq, sendo, qbuf, kbuf, qin, qord, kord, kob, acc, ans, perm,
    local_sem, send_sem, q_sem, k_sem, qo_sem, ko_sem, back_sem,
):
    y = lax.axis_index("grp")
    shard = lax.axis_index("shard")
    x, z, c = shard // 8, (shard // 2) % 4, shard % 2

    def device(dx=0, dy=0, dz=0, dc=0):
        return (
            (y + dy) % 4,
            (((x + dx) % 4) * 4 + (z + dz) % 4) * 2 + (c + dc) % 2,
        )

    started = []

    def send(src, dst, sem, to):
        copy = pltpu.make_async_remote_copy(
            src_ref=src,
            dst_ref=dst,
            send_sem=send_sem.at[len(started)],
            recv_sem=sem,
            device_id=to,
            device_id_type=MESH,
        )
        copy.start()
        started.append(copy)

    def arrived(dst, sem):
        pltpu.make_async_remote_copy(
            src_ref=dst,
            dst_ref=dst,
            send_sem=send_sem.at[0],
            recv_sem=sem,
            device_id=device(dc=1),
            device_id_type=MESH,
        ).wait_recv()

    def q_half(place, h):
        slot = Q_SLOT[place]
        return qbuf.at[pl.ds(slot * CH + h * HALF, HALF), :], q_sem.at[2 * slot + h]

    def k_part(place, h=None):
        row = K_ROW[place + (h or 0,)]
        return kbuf.at[pl.ds(row, CH if h is None else HALF), :], k_sem.at[row // HALF]

    barrier = pltpu.get_barrier_semaphore()
    near = [{"dx": 1}, {"dx": 3}, {"dy": 1}, {"dy": 2}, {"dy": 3}, {"dz": 1}, {"dz": 3}, {"dc": 1}]
    for place in near:
        pl.semaphore_signal(barrier, inc=1, device_id=device(**place), device_id_type=MESH)


    loads = [
        pltpu.make_async_copy(src, dst, local_sem.at[i])
        for i, (src, dst) in enumerate(
            (
                (scales_hbm, scales_ref),
                (offsets_hbm, offsets_ref),
                (codes_hbm.at[pl.ds(0, CH), :], codes.at[pl.ds(0, CH), :]),
                (counts_hbm, counts_ref),
                (key_order_hbm, key_order_ref),
                (ids_hbm, ids_ref),
                (order_hbm, order_ref),
                (rows_hbm, rows),
                *((codes_hbm.at[pl.ds(j * CH, CH), :], codes.at[pl.ds(j * CH, CH), :]) for j in J_ORDER[1:]),
            )
        )
    ]
    for load in loads:
        load.start()

    def decode(i):
        j = J_ORDER[i]
        if i:
            loads[7 + i].wait()
        decoded = (
            codes[pl.ds(j * CH, CH), :].astype(jnp.float32) * scales_ref[j // 2 : j // 2 + 1, :]
            + offsets_ref[j // 2 : j // 2 + 1, :]
        )
        kbuf[pl.ds(K_ROW[0, 0, j, 0], CH), :] = (
            decoded * lax.rsqrt(jnp.sum(decoded * decoded, axis=-1, keepdims=True) + epsilon)
        ).astype(jnp.bfloat16)

    def spread(j):
        here, _ = k_part((0, 0, j))
        for to, place in (
            (device(dz=1), (3, 0, j)),
            (device(dz=3), (1, 0, j)),
            (device(dc=1), (0, 1, j)),
        ):
            send(here, *k_part(place), to)

    def keys_order(dz, dc):
        return kord.at[dc * 4 + dz], ko_sem.at[dc * 4 + dz]

    for load in loads[:5]:
        load.wait()
    for j in range(4):
        place = shard * 256 + (j % 2) * CH + lax.broadcasted_iota(jnp.int32, (1, CH), 1)
        live = place < counts_ref[j // 2]
        kord[0, j : j + 1, :] = jnp.where(
            live, key_order_ref[j // 2 : j // 2 + 1, (j % 2) * CH : (j % 2 + 1) * CH], DEAD
        )

    decode(0)

    pl.semaphore_wait(barrier, len(near))

    here, _ = keys_order(0, 0)
    send(here, *keys_order(3, 0), device(dz=1))
    send(here, *keys_order(1, 0), device(dz=3))
    send(here, *keys_order(0, 1), device(dc=1))
    spread(J_ORDER[0])

    n_rows = rows.shape[0]
    for load in loads[5:7]:
        load.wait()
    ids = ids_ref[...]
    target = (ids // 2 - y + 4) % 4
    groups = lax.broadcasted_iota(jnp.int32, (16, n_rows), 0)
    onehot = jnp.where(groups == target, 1.0, 0.0)
    before = lax.broadcasted_iota(jnp.int32, (n_rows, n_rows), 0) < lax.broadcasted_iota(
        jnp.int32, (n_rows, n_rows), 1
    )
    earlier = jnp.dot(
        onehot.astype(jnp.bfloat16),
        jnp.where(before, 1.0, 0.0).astype(jnp.bfloat16),
        preferred_element_type=jnp.float32,
    )
    position = jnp.sum(
        onehot * (earlier + (groups * CH).astype(jnp.float32)), axis=0, keepdims=True
    ).astype(jnp.int32)
    slots = lax.broadcasted_iota(jnp.int32, (4 * CH, n_rows), 0)
    perm[...] = jnp.where(slots == position, 1.0, 0.0).astype(jnp.bfloat16)

    order = order_ref[...]
    pieces = []
    for cluster in range(2):
        own = jnp.where(ids % 2 == cluster, order, 0)
        pieces += [(own >> (8 * p)) & 255 for p in range(4)]
    pieces = jnp.concatenate(pieces + pieces, axis=0).astype(jnp.float32).astype(jnp.bfloat16)
    moved = lax.dot_general(
        pieces, perm[...], (((1,), (1,)), ((), ())), preferred_element_type=jnp.float32
    ).astype(jnp.int32)
    for d in range(4):
        for cluster in range(2):
            part = moved[4 * cluster : 4 * cluster + 4, d * CH : (d + 1) * CH]
            joined = part[0:1] + part[1:2] * 256 + part[2:3] * 65536 + part[3:4] * 16777216
            if d == 0:
                qin[0, 0, cluster : cluster + 1, :] = joined
            else:
                sendo[d, cluster : cluster + 1, :] = joined
    loads[7].wait()
    values = rows[...].astype(jnp.float32)
    queries = (
        values * lax.rsqrt(jnp.sum(values * values, axis=-1, keepdims=True) + epsilon)
    ).astype(jnp.bfloat16)

    def picked(d):
        return jnp.dot(
            perm[pl.ds(d * CH, CH), :], queries, preferred_element_type=jnp.float32
        ).astype(jnp.bfloat16)

    qbuf[pl.ds(0, CH), :] = picked(0)
    for d in range(1, 4):
        sendq[d] = picked(d)

    def send_x(dy, h):
        here, _ = q_half((0, dy), h)
        for dx, there in ((1, 3), (3, 1)):
            send(here, *q_half((there, dy), h), device(dx=dx))

    def send_y(d, h):
        send(sendq.at[d, pl.ds(h * HALF, HALF)], *q_half((0, (4 - d) % 4), h), device(dy=d))

    for d in range(1, 4):
        send(sendo.at[d], qin.at[0, 4 - d], qo_sem.at[0], device(dy=d))
    for h in range(2):
        for d in (1, 3):
            send_y(d, h)
        send_x(0, h)
    for i in range(1, 4):
        decode(i)
        spread(J_ORDER[i])

    arrived(qin.at[0, pl.ds(1, 3)], qo_sem.at[0])
    send(qin.at[0], qin.at[3], qo_sem.at[3], device(dx=1))
    send(qin.at[0], qin.at[1], qo_sem.at[1], device(dx=3))
    for dz in (3, 1):
        arrived(*keys_order(dz, 0))
        send(keys_order(dz, 0)[0], *keys_order(dz, 1), device(dc=1))
    send(keys_order(3, 0)[0], *keys_order(2, 0), device(dz=1))

    def spread_orders(dz, dc):
        for j in range(4):
            turned = jnp.broadcast_to(kord[dc * 4 + dz, j : j + 1, :], (CH, CH)).T
            for h in range(2):
                kob[pl.ds(K_ROW[dz, dc, j, h], HALF), :] = turned[h * HALF : (h + 1) * HALF]

    def place_orders(dx):
        for dy in range(4):
            qord[Q_SLOT[dx, dy]] = qin[dx, dy]

    acc[...] = jnp.zeros_like(acc)
    place_orders(0)
    for dz in (0, 3, 1):
        spread_orders(dz, 0)
        arrived(*keys_order(dz, 1))
        spread_orders(dz, 1)

    def tile(key_row, n_keys, block, n_blocks):
        keys = kbuf[pl.ds(pl.multiple_of(key_row, 2 * CH), n_keys), :]
        asks = qbuf[pl.ds(pl.multiple_of(block * CH, CH), n_blocks * CH), :]
        return lax.dot_general(
            keys, asks, (((1,), (1,)), ((), ())), preferred_element_type=jnp.float32
        )

    def keep(key_row, n_keys, block, n_blocks, scores):
        key_order = kob[pl.ds(pl.multiple_of(key_row, 2 * CH), n_keys), :]
        cluster = (key_row // (4 * CH)) % 2
        for h in range(n_blocks):
            limit = qord[block + h, pl.ds(cluster, 1), :]
            part = jnp.where(key_order < limit, scores[:, h * CH : (h + 1) * CH], 0.0)
            best = jnp.max(part.reshape(n_keys // 8, 8, CH), axis=0)
            acc[block + h] = jnp.maximum(acc[block + h], best)

    def tiles(*items):
        scores = [tile(*item) for item in items]
        for item, found in zip(items, scores):
            keep(*item, found)

    def work(count, place, n_keys, n_blocks, together):
        def some(first, size):
            at = [place(first + i) for i in range(size)]
            scores = [tile(row, n_keys, block, n_blocks) for row, block in at]
            for (row, block), found in zip(at, scores):
                keep(row, n_keys, block, n_blocks, found)

        def step(i, carry):
            some(together * i, together)
            return carry

        lax.fori_loop(0, count // together, step, 0)
        if count % together:
            some(count - count % together, count % together)

    def new_queries(qt, n_qt, n_kt):
        work(
            n_kt * n_qt, lambda i: ((i % n_kt) * 4 * CH, (qt + i // n_kt) * 2), 4 * CH, 2, 2
        )

    def new_keys(row, n_keys, n_qt):
        work(n_qt // 2, lambda i: (row, i * 4), n_keys, 4, 1)
        if n_qt % 2:
            work(1, lambda i: (row, (n_qt - 1) * 2), n_keys, 2, 1)

    def other_core(place, h=None):
        dz, _, j = place
        send(k_part(place, h)[0], *k_part((dz, 1, j), h), device(dc=1))

    def got_keys(*places, h=None):
        for place in places:
            arrived(*k_part(place, h))

    def got_queries(place, h):
        arrived(*q_half(place, h))

    def give_back(places):
        for dx, dy in places:
            slot = Q_SLOT[(4 - dx) % 4, (4 - dy) % 4]
            send(acc.at[Q_SLOT[dx, dy]], ans.at[slot], back_sem.at[0], device(dx=dx, dy=dy))

    for tick in range(1, 7):
        if tick <= 4:
            j, dy = J_ORDER[tick - 1], DY_ORDER[tick - 1]
            for ready in {1: (3, 1), 2: (2,)}.get(tick, ()):
                for h in range(2):
                    got_queries((0, ready), h)
                    send_x(ready, h)
            if tick == 1:
                for h in range(2):
                    send_y(2, h)
            got_keys((3, 0, j), (1, 0, j))
            side, to = ((3, 1), (1, 3))[j % 2]
            if j < 2:
                send(k_part((side, 0, j))[0], *k_part((2, 0, j)), device(dz=to))
            else:
                for h in range(2):
                    row = K_ROW[side, 0, j, h]
                    send(kbuf.at[pl.ds(row, HALF), :], *k_part((2, 0, j), h), device(dz=to))
            other_core((3, 0, j))
            other_core((1, 0, j))
            for h in range(2):
                got_queries((3, dy), h)
                got_queries((1, dy), h)
            for passed in {2: (0, 3), 3: (1,), 4: (2,)}.get(tick, ()):
                side, to = (3, 1) if passed in (0, 1) else (1, 3)
                for h in range(2):
                    send(
                        q_half((side, passed), h)[0], *q_half((2, passed), h), device(dx=to)
                    )
            if tick == 1:
                for dx in (3, 1):
                    arrived(qin.at[dx], qo_sem.at[dx])
                    place_orders(dx)
                send(qin.at[3], qin.at[2], qo_sem.at[2], device(dx=1))
                got_keys(*((0, 1, own) for own in J_ORDER))
                new_queries(0, 2, 2)
                n_q = 2
            elif tick == 2:
                new_queries(2, 2, 3)
                n_q = 4
            else:
                new_queries(tick + 1, 1, tick + 1)
                n_q = tick + 2
            got_keys((3, 1, j), (1, 1, j))
            if tick == 4:
                arrived(*keys_order(2, 0))
                send(keys_order(2, 0)[0], *keys_order(2, 1), device(dc=1))
            new_keys((tick + 1) * 4 * CH, 4 * CH, n_q)
            if tick == 4:
                arrived(qin.at[2], qo_sem.at[2])
                place_orders(2)
                spread_orders(2, 0)
                arrived(*keys_order(2, 1))
                spread_orders(2, 1)
        elif tick == 5:
            got_keys((2, 0, 0), (2, 0, 1))
            other_core((2, 0, 0))
            other_core((2, 0, 1))
            for dy in (0, 3):
                for h in range(2):
                    got_queries((2, dy), h)
            tiles(*((kt * 4 * CH, 4 * CH, 12, 2) for kt in range(6)))
            got_keys((2, 1, 0), (2, 1, 1))
            tiles((6 * 4 * CH, 4 * CH, 0, 14))
        else:
            last = 7 * 4 * CH
            got_keys((2, 0, 2), (2, 0, 3), h=0)
            other_core((2, 0, 2), 0)
            other_core((2, 0, 3), 0)
            got_keys((2, 1, 2), (2, 1, 3), h=0)
            tiles((last, 2 * CH, 0, 14))
            got_keys((2, 0, 2), (2, 0, 3), h=1)
            other_core((2, 0, 2), 1)
            other_core((2, 0, 3), 1)
            for dy in (1, 2):
                for h in range(2):
                    got_queries((2, dy), h)
            tiles(
                *((kt * 4 * CH, 4 * CH, 14, 2) for kt in range(7)), (last, 2 * CH, 14, 2)
            )
            got_keys((2, 1, 2), (2, 1, 3), h=1)
            tiles((last + 2 * CH, 2 * CH, 8, 8))
            give_back(Q_ORDER[:7:-1])
            tiles((last + 2 * CH, 2 * CH, 0, 8))
            give_back(Q_ORDER[1:8])

    arrived(ans.at[pl.ds(1, 15)], back_sem.at[0])
    answers = []
    for d in range(4):
        best = acc[0] if d == 0 else ans[Q_SLOT[0, d]]
        for dx in range(1, 4):
            best = jnp.maximum(best, ans[Q_SLOT[dx, d]])
        answers.append(jnp.max(best, axis=0, keepdims=True))
    answer = jnp.concatenate(answers, axis=1)
    high = answer.astype(jnp.bfloat16).astype(jnp.float32)
    middle = (answer - high).astype(jnp.bfloat16).astype(jnp.float32)
    low = answer - high - middle
    parts = jnp.concatenate([high, middle, low, jnp.zeros((13, 4 * CH), jnp.float32)], axis=0)
    back = jnp.dot(parts.astype(jnp.bfloat16), perm[...], preferred_element_type=jnp.float32)
    out_ref[...] = back[0:8]
    for copy in started:
        copy.wait_send()


def per_device(new_rows, cluster_ids, new_order, codes, scales, offsets, counts, earlier_order):
    n_rows, width = new_rows.shape
    vmem = pl.BlockSpec(memory_space=pltpu.VMEM)
    n_q, n_k = len(Q_ORDER), len(K_ORDER)
    out = pl.pallas_call(
        kernel,
        out_shape=jax.ShapeDtypeStruct((8, n_rows), jnp.float32),
        in_specs=[pl.BlockSpec(memory_space=pl.ANY)] * 8,
        out_specs=vmem,
        scratch_shapes=[
            pltpu.VMEM((n_rows, width), jnp.bfloat16),
            pltpu.VMEM((1, n_rows), jnp.int32),
            pltpu.VMEM((1, n_rows), jnp.int32),
            pltpu.VMEM((4 * CH, width), jnp.bfloat16),
            pltpu.VMEM((2, width), jnp.float32),
            pltpu.VMEM((2, width), jnp.float32),
            pltpu.SMEM((2,), jnp.int32),
            pltpu.VMEM((2, 2 * CH), jnp.int32),
            pltpu.VMEM((4, CH, width), jnp.bfloat16),
            pltpu.VMEM((4, 2, CH), jnp.int32),
            pltpu.VMEM((n_q * CH, width), jnp.bfloat16),
            pltpu.VMEM((n_k * CH, width), jnp.bfloat16),
            pltpu.VMEM((4, 4, 2, CH), jnp.int32),
            pltpu.VMEM((n_q, 2, CH), jnp.int32),
            pltpu.VMEM((8, 4, CH), jnp.int32),
            pltpu.VMEM((n_k * CH, CH), jnp.int32),
            pltpu.VMEM((n_q, 8, CH), jnp.float32),
            pltpu.VMEM((n_q, 8, CH), jnp.float32),
            pltpu.VMEM((4 * CH, n_rows), jnp.bfloat16),
            pltpu.SemaphoreType.DMA((11,)),
            pltpu.SemaphoreType.DMA((128,)),
            pltpu.SemaphoreType.DMA((2 * n_q,)),
            pltpu.SemaphoreType.DMA((2 * n_k,)),
            pltpu.SemaphoreType.DMA((4,)),
            pltpu.SemaphoreType.DMA((8,)),
            pltpu.SemaphoreType.DMA((1,)),
        ],
        compiler_params=pltpu.CompilerParams(
            collective_id=0, has_side_effects=True, vmem_limit_bytes=63 * 2**20
        ),
        cost_estimate=pl.CostEstimate(
            flops=2 * n_q * n_k * CH * CH * width, bytes_accessed=2**21, transcendentals=1024
        ),
    )(
        new_rows,
        cluster_ids.reshape(1, n_rows),
        new_order.reshape(1, n_rows),
        codes.reshape(4 * CH, width),
        scales,
        offsets,
        counts,
        earlier_order,
    )
    return out[0] + out[1] + out[2]


def solution(mesh):
    return jax.shard_map(
        per_device,
        mesh=mesh,
        in_specs=(
            P(("grp", "shard"), None),
            P(("grp", "shard")),
            P(("grp", "shard")),
            P("grp", "shard", None),
            P("grp", None),
            P("grp", None),
            P("grp"),
            P("grp", "shard"),
        ),
        out_specs=P(("grp", "shard")),
        check_vma=False,
    )
```

```python
import functools

import jax
import jax.numpy as jnp
from jax import lax
from jax.experimental import pallas as pl
from jax.experimental.pallas import tpu as pltpu
from jax.sharding import PartitionSpec as P

MESH = pl.DeviceIdType.MESH
epsilon = 1e-06
DEAD = 2147483647
CH = 128
HALF = CH // 2

Q_ORDER = [
    (0, 0), (0, 3),
    (3, 0), (1, 0),
    (0, 1), (0, 2),
    (3, 3), (1, 3),
    (3, 1), (1, 1),
    (3, 2), (1, 2),
    (2, 0), (2, 3),
    (2, 1), (2, 2),
]
Q_SLOT = {place: i for i, place in enumerate(Q_ORDER)}
K_ORDER = [
    (0, 0, 0), (0, 0, 1), (0, 1, 0), (0, 1, 1),
    (0, 0, 2), (0, 0, 3), (0, 1, 2), (0, 1, 3),
]
J_ORDER = [0, 2, 1, 3]
for _j in J_ORDER:
    K_ORDER += [(3, 0, _j), (3, 1, _j), (1, 0, _j), (1, 1, _j)]
for _j in (0, 2):
    K_ORDER += [(2, 0, _j), (2, 1, _j), (2, 0, _j + 1), (2, 1, _j + 1)]
K_ROW = {
    place + (h,): i * CH + h * HALF if i < 28 else 28 * CH + h * 4 * HALF + (i - 28) * HALF
    for i, place in enumerate(K_ORDER)
    for h in range(2)
}
DY_ORDER = [0, 3, 1, 2]


def kernel(
    rows_hbm, ids_hbm, order_hbm, codes_hbm, scales_hbm, offsets_hbm, counts_hbm, key_order_hbm,
    out_ref,
    rows, ids_ref, order_ref, codes, scales_ref, offsets_ref, counts_ref, key_order_ref,
    sendq, sendo, qbuf, kbuf, qin, qord, kord, kob, acc, ans, perm,
    local_sem, send_sem, q_sem, k_sem, qo_sem, ko_sem, back_sem,
):
    y = lax.axis_index("grp")
    shard = lax.axis_index("shard")
    x, z, c = shard // 8, (shard // 2) % 4, shard % 2

    def device(dx=0, dy=0, dz=0, dc=0):
        return (
            (y + dy) % 4,
            (((x + dx) % 4) * 4 + (z + dz) % 4) * 2 + (c + dc) % 2,
        )

    started = []

    def send(src, dst, sem, to):
        copy = pltpu.make_async_remote_copy(
            src_ref=src,
            dst_ref=dst,
            send_sem=send_sem.at[len(started)],
            recv_sem=sem,
            device_id=to,
            device_id_type=MESH,
        )
        copy.start()
        started.append(copy)

    def arrived(dst, sem):
        pltpu.make_async_remote_copy(
            src_ref=dst,
            dst_ref=dst,
            send_sem=send_sem.at[0],
            recv_sem=sem,
            device_id=device(dc=1),
            device_id_type=MESH,
        ).wait_recv()

    def q_half(place, h):
        slot = Q_SLOT[place]
        return qbuf.at[pl.ds(slot * CH + h * HALF, HALF), :], q_sem.at[2 * slot + h]

    def k_part(place, h=None):
        row = K_ROW[place + (h or 0,)]
        return kbuf.at[pl.ds(row, CH if h is None else HALF), :], k_sem.at[row // HALF]

    barrier = pltpu.get_barrier_semaphore()
    near = [{"dx": 1}, {"dx": 3}, {"dy": 1}, {"dy": 2}, {"dy": 3}, {"dz": 1}, {"dz": 3}, {"dc": 1}]
    for place in near:
        pl.semaphore_signal(barrier, inc=1, device_id=device(**place), device_id_type=MESH)


    loads = [
        pltpu.make_async_copy(src, dst, local_sem.at[i])
        for i, (src, dst) in enumerate(
            (
                (scales_hbm, scales_ref),
                (offsets_hbm, offsets_ref),
                (codes_hbm.at[pl.ds(0, CH), :], codes.at[pl.ds(0, CH), :]),
                (counts_hbm, counts_ref),
                (key_order_hbm, key_order_ref),
                (ids_hbm, ids_ref),
                (order_hbm, order_ref),
                (rows_hbm, rows),
                *((codes_hbm.at[pl.ds(j * CH, CH), :], codes.at[pl.ds(j * CH, CH), :]) for j in J_ORDER[1:]),
            )
        )
    ]
    for load in loads:
        load.start()

    def decode(i):
        j = J_ORDER[i]
        if i:
            loads[7 + i].wait()
        decoded = (
            codes[pl.ds(j * CH, CH), :].astype(jnp.float32) * scales_ref[j // 2 : j // 2 + 1, :]
            + offsets_ref[j // 2 : j // 2 + 1, :]
        )
        kbuf[pl.ds(K_ROW[0, 0, j, 0], CH), :] = (
            decoded * lax.rsqrt(jnp.sum(decoded * decoded, axis=-1, keepdims=True) + epsilon)
        ).astype(jnp.bfloat16)

    def spread(j):
        here, _ = k_part((0, 0, j))
        for to, place in (
            (device(dz=1), (3, 0, j)),
            (device(dz=3), (1, 0, j)),
            (device(dc=1), (0, 1, j)),
        ):
            send(here, *k_part(place), to)

    def keys_order(dz, dc):
        return kord.at[dc * 4 + dz], ko_sem.at[dc * 4 + dz]

    for load in loads[:5]:
        load.wait()
    for j in range(4):
        place = shard * 256 + (j % 2) * CH + lax.broadcasted_iota(jnp.int32, (1, CH), 1)
        live = place < counts_ref[j // 2]
        kord[0, j : j + 1, :] = jnp.where(
            live, key_order_ref[j // 2 : j // 2 + 1, (j % 2) * CH : (j % 2 + 1) * CH], DEAD
        )

    decode(0)

    pl.semaphore_wait(barrier, len(near))

    here, _ = keys_order(0, 0)
    send(here, *keys_order(3, 0), device(dz=1))
    send(here, *keys_order(1, 0), device(dz=3))
    send(here, *keys_order(0, 1), device(dc=1))
    spread(J_ORDER[0])

    n_rows = rows.shape[0]
    for load in loads[5:7]:
        load.wait()
    ids = ids_ref[...]
    target = (ids // 2 - y + 4) % 4
    groups = lax.broadcasted_iota(jnp.int32, (16, n_rows), 0)
    onehot = jnp.where(groups == target, 1.0, 0.0)
    before = lax.broadcasted_iota(jnp.int32, (n_rows, n_rows), 0) < lax.broadcasted_iota(
        jnp.int32, (n_rows, n_rows), 1
    )
    earlier = jnp.dot(
        onehot.astype(jnp.bfloat16),
        jnp.where(before, 1.0, 0.0).astype(jnp.bfloat16),
        preferred_element_type=jnp.float32,
    )
    position = jnp.sum(
        onehot * (earlier + (groups * CH).astype(jnp.float32)), axis=0, keepdims=True
    ).astype(jnp.int32)
    slots = lax.broadcasted_iota(jnp.int32, (4 * CH, n_rows), 0)
    perm[...] = jnp.where(slots == position, 1.0, 0.0).astype(jnp.bfloat16)

    order = order_ref[...]
    pieces = []
    for cluster in range(2):
        own = jnp.where(ids % 2 == cluster, order, 0)
        pieces += [(own >> (8 * p)) & 255 for p in range(4)]
    pieces = jnp.concatenate(pieces + pieces, axis=0).astype(jnp.float32).astype(jnp.bfloat16)
    moved = lax.dot_general(
        pieces, perm[...], (((1,), (1,)), ((), ())), preferred_element_type=jnp.float32
    ).astype(jnp.int32)
    for d in range(4):
        for cluster in range(2):
            part = moved[4 * cluster : 4 * cluster + 4, d * CH : (d + 1) * CH]
            joined = part[0:1] + part[1:2] * 256 + part[2:3] * 65536 + part[3:4] * 16777216
            if d == 0:
                qin[0, 0, cluster : cluster + 1, :] = joined
            else:
                sendo[d, cluster : cluster + 1, :] = joined
    loads[7].wait()
    values = rows[...].astype(jnp.float32)
    queries = (
        values * lax.rsqrt(jnp.sum(values * values, axis=-1, keepdims=True) + epsilon)
    ).astype(jnp.bfloat16)

    def picked(d):
        return jnp.dot(
            perm[pl.ds(d * CH, CH), :], queries, preferred_element_type=jnp.float32
        ).astype(jnp.bfloat16)

    def send_x(dy, h):
        here, _ = q_half((0, dy), h)
        for dx, there in ((1, 3), (3, 1)):
            send(here, *q_half((there, dy), h), device(dx=dx))

    def send_y(d, h):
        send(sendq.at[d, pl.ds(h * HALF, HALF)], *q_half((0, (4 - d) % 4), h), device(dy=d))

    for d in range(1, 4):
        send(sendo.at[d], qin.at[0, 4 - d], qo_sem.at[0], device(dy=d))
    qbuf[pl.ds(0, CH), :] = picked(0)
    for h in range(2):
        send_x(0, h)
    for d in (1, 3, 2):
        sendq[d] = picked(d)
    for h in range(2):
        for d in (1, 3):
            send_y(d, h)
    for i in range(1, 4):
        decode(i)
        spread(J_ORDER[i])

    arrived(qin.at[0, pl.ds(1, 3)], qo_sem.at[0])
    send(qin.at[0], qin.at[3], qo_sem.at[3], device(dx=1))
    send(qin.at[0], qin.at[1], qo_sem.at[1], device(dx=3))
    for dz in (3, 1):
        arrived(*keys_order(dz, 0))
        send(keys_order(dz, 0)[0], *keys_order(dz, 1), device(dc=1))
    send(keys_order(3, 0)[0], *keys_order(2, 0), device(dz=1))

    def spread_orders(dz, dc):
        for j in range(4):
            turned = jnp.broadcast_to(kord[dc * 4 + dz, j : j + 1, :], (CH, CH)).T
            for h in range(2):
                kob[pl.ds(K_ROW[dz, dc, j, h], HALF), :] = turned[h * HALF : (h + 1) * HALF]

    def place_orders(dx):
        for dy in range(4):
            qord[Q_SLOT[dx, dy]] = qin[dx, dy]

    acc[...] = jnp.zeros_like(acc)
    place_orders(0)
    for dz in (0, 3, 1):
        spread_orders(dz, 0)
        arrived(*keys_order(dz, 1))
        spread_orders(dz, 1)

    def tile(key_row, n_keys, block, n_blocks):
        keys = kbuf[pl.ds(pl.multiple_of(key_row, 2 * CH), n_keys), :]
        asks = qbuf[pl.ds(pl.multiple_of(block * CH, CH), n_blocks * CH), :]
        return lax.dot_general(
            keys, asks, (((1,), (1,)), ((), ())), preferred_element_type=jnp.float32
        )

    def keep(key_row, n_keys, block, n_blocks, scores):
        key_order = kob[pl.ds(pl.multiple_of(key_row, 2 * CH), n_keys), :]
        cluster = (key_row // (4 * CH)) % 2
        for h in range(n_blocks):
            limit = qord[block + h, pl.ds(cluster, 1), :]
            part = jnp.where(key_order < limit, scores[:, h * CH : (h + 1) * CH], 0.0)
            best = jnp.max(part.reshape(n_keys // 8, 8, CH), axis=0)
            acc[block + h] = jnp.maximum(acc[block + h], best)

    def tiles(*items):
        scores = [tile(*item) for item in items]
        for item, found in zip(items, scores):
            keep(*item, found)

    def work(count, place, n_keys, n_blocks, together):
        def some(first, size):
            at = [place(first + i) for i in range(size)]
            scores = [tile(row, n_keys, block, n_blocks) for row, block in at]
            for (row, block), found in zip(at, scores):
                keep(row, n_keys, block, n_blocks, found)

        def step(i, carry):
            some(together * i, together)
            return carry

        lax.fori_loop(0, count // together, step, 0)
        if count % together:
            some(count - count % together, count % together)

    def new_queries(qt, n_qt, n_kt):
        work(
            n_kt * n_qt, lambda i: ((i % n_kt) * 4 * CH, (qt + i // n_kt) * 2), 4 * CH, 2, 2
        )

    def new_keys(row, n_keys, n_qt):
        work(n_qt // 2, lambda i: (row, i * 4), n_keys, 4, 1)
        if n_qt % 2:
            work(1, lambda i: (row, (n_qt - 1) * 2), n_keys, 2, 1)

    def other_core(place, h=None):
        dz, _, j = place
        send(k_part(place, h)[0], *k_part((dz, 1, j), h), device(dc=1))

    def got_keys(*places, h=None):
        for place in places:
            arrived(*k_part(place, h))

    def got_queries(place, h):
        arrived(*q_half(place, h))

    def give_back(places):
        for dx, dy in places:
            slot = Q_SLOT[(4 - dx) % 4, (4 - dy) % 4]
            send(acc.at[Q_SLOT[dx, dy]], ans.at[slot], back_sem.at[0], device(dx=dx, dy=dy))

    for tick in range(1, 7):
        if tick <= 4:
            j, dy = J_ORDER[tick - 1], DY_ORDER[tick - 1]
            for ready in {1: (3, 1), 2: (2,)}.get(tick, ()):
                for h in range(2):
                    got_queries((0, ready), h)
                    send_x(ready, h)
            if tick == 1:
                for h in range(2):
                    send_y(2, h)
            got_keys((3, 0, j), (1, 0, j))
            side, to = ((3, 1), (1, 3))[j % 2]
            if j < 2:
                send(k_part((side, 0, j))[0], *k_part((2, 0, j)), device(dz=to))
            else:
                for h in range(2):
                    row = K_ROW[side, 0, j, h]
                    send(kbuf.at[pl.ds(row, HALF), :], *k_part((2, 0, j), h), device(dz=to))
            other_core((3, 0, j))
            other_core((1, 0, j))
            for h in range(2):
                got_queries((3, dy), h)
                got_queries((1, dy), h)
            for passed in {2: (0, 3), 3: (1,), 4: (2,)}.get(tick, ()):
                side, to = (3, 1) if passed in (0, 1) else (1, 3)
                for h in range(2):
                    send(
                        q_half((side, passed), h)[0], *q_half((2, passed), h), device(dx=to)
                    )
            if tick == 1:
                for dx in (3, 1):
                    arrived(qin.at[dx], qo_sem.at[dx])
                    place_orders(dx)
                send(qin.at[3], qin.at[2], qo_sem.at[2], device(dx=1))
                got_keys(*((0, 1, own) for own in J_ORDER))
                new_queries(0, 2, 2)
                n_q = 2
            elif tick == 2:
                new_queries(2, 2, 3)
                n_q = 4
            else:
                new_queries(tick + 1, 1, tick + 1)
                n_q = tick + 2
            got_keys((3, 1, j), (1, 1, j))
            if tick == 4:
                arrived(*keys_order(2, 0))
                send(keys_order(2, 0)[0], *keys_order(2, 1), device(dc=1))
            new_keys((tick + 1) * 4 * CH, 4 * CH, n_q)
            if tick == 4:
                arrived(qin.at[2], qo_sem.at[2])
                place_orders(2)
                spread_orders(2, 0)
                arrived(*keys_order(2, 1))
                spread_orders(2, 1)
        elif tick == 5:
            got_keys((2, 0, 0), (2, 0, 1))
            other_core((2, 0, 0))
            other_core((2, 0, 1))
            for dy in (0, 3):
                for h in range(2):
                    got_queries((2, dy), h)
            tiles(*((kt * 4 * CH, 4 * CH, 12, 2) for kt in range(6)))
            got_keys((2, 1, 0), (2, 1, 1))
            tiles((6 * 4 * CH, 4 * CH, 0, 8))
            got_keys((2, 0, 2), (2, 0, 3), h=0)
            other_core((2, 0, 2), 0)
            other_core((2, 0, 3), 0)
            tiles((6 * 4 * CH, 4 * CH, 8, 6))
        else:
            last = 7 * 4 * CH
            got_keys((2, 1, 2), (2, 1, 3), h=0)
            tiles((last, 2 * CH, 0, 14))
            got_keys((2, 0, 2), (2, 0, 3), h=1)
            other_core((2, 0, 2), 1)
            other_core((2, 0, 3), 1)
            for dy in (1, 2):
                for h in range(2):
                    got_queries((2, dy), h)
            tiles(
                *((kt * 4 * CH, 4 * CH, 14, 2) for kt in range(7)), (last, 2 * CH, 14, 2)
            )
            got_keys((2, 1, 2), (2, 1, 3), h=1)
            tiles((last + 2 * CH, 2 * CH, 8, 8))
            give_back(Q_ORDER[:7:-1])
            tiles((last + 2 * CH, 2 * CH, 0, 8))
            give_back(Q_ORDER[1:8])

    for copy in started[:-15]:
        copy.wait_send()
    arrived(ans.at[pl.ds(1, 15)], back_sem.at[0])
    answers = []
    for d in range(4):
        best = acc[0] if d == 0 else ans[Q_SLOT[0, d]]
        for dx in range(1, 4):
            best = jnp.maximum(best, ans[Q_SLOT[dx, d]])
        answers.append(jnp.max(best, axis=0, keepdims=True))
    answer = jnp.concatenate(answers, axis=1)
    high = answer.astype(jnp.bfloat16).astype(jnp.float32)
    middle = (answer - high).astype(jnp.bfloat16).astype(jnp.float32)
    low = answer - high - middle
    parts = jnp.concatenate([high, middle, low, jnp.zeros((13, 4 * CH), jnp.float32)], axis=0)
    back = jnp.dot(parts.astype(jnp.bfloat16), perm[...], preferred_element_type=jnp.float32)
    out_ref[...] = back[0:8]
    for copy in started[-15:]:
        copy.wait_send()


def per_device(new_rows, cluster_ids, new_order, codes, scales, offsets, counts, earlier_order):
    n_rows, width = new_rows.shape
    vmem = pl.BlockSpec(memory_space=pltpu.VMEM)
    n_q, n_k = len(Q_ORDER), len(K_ORDER)
    out = pl.pallas_call(
        kernel,
        out_shape=jax.ShapeDtypeStruct((8, n_rows), jnp.float32),
        in_specs=[pl.BlockSpec(memory_space=pl.ANY)] * 8,
        out_specs=vmem,
        scratch_shapes=[
            pltpu.VMEM((n_rows, width), jnp.bfloat16),
            pltpu.VMEM((1, n_rows), jnp.int32),
            pltpu.VMEM((1, n_rows), jnp.int32),
            pltpu.VMEM((4 * CH, width), jnp.bfloat16),
            pltpu.VMEM((2, width), jnp.float32),
            pltpu.VMEM((2, width), jnp.float32),
            pltpu.SMEM((2,), jnp.int32),
            pltpu.VMEM((2, 2 * CH), jnp.int32),
            pltpu.VMEM((4, CH, width), jnp.bfloat16),
            pltpu.VMEM((4, 2, CH), jnp.int32),
            pltpu.VMEM((n_q * CH, width), jnp.bfloat16),
            pltpu.VMEM((n_k * CH, width), jnp.bfloat16),
            pltpu.VMEM((4, 4, 2, CH), jnp.int32),
            pltpu.VMEM((n_q, 2, CH), jnp.int32),
            pltpu.VMEM((8, 4, CH), jnp.int32),
            pltpu.VMEM((n_k * CH, CH), jnp.int32),
            pltpu.VMEM((n_q, 8, CH), jnp.float32),
            pltpu.VMEM((n_q, 8, CH), jnp.float32),
            pltpu.VMEM((4 * CH, n_rows), jnp.bfloat16),
            pltpu.SemaphoreType.DMA((11,)),
            pltpu.SemaphoreType.DMA((128,)),
            pltpu.SemaphoreType.DMA((2 * n_q,)),
            pltpu.SemaphoreType.DMA((2 * n_k,)),
            pltpu.SemaphoreType.DMA((4,)),
            pltpu.SemaphoreType.DMA((8,)),
            pltpu.SemaphoreType.DMA((1,)),
        ],
        compiler_params=pltpu.CompilerParams(
            collective_id=0, has_side_effects=True, vmem_limit_bytes=63 * 2**20
        ),
        cost_estimate=pl.CostEstimate(
            flops=2 * n_q * n_k * CH * CH * width, bytes_accessed=2**21, transcendentals=1024
        ),
    )(
        new_rows,
        cluster_ids.reshape(1, n_rows),
        new_order.reshape(1, n_rows),
        codes.reshape(4 * CH, width),
        scales,
        offsets,
        counts,
        earlier_order,
    )
    return out[0] + out[1] + out[2]


def solution(mesh):
    return jax.shard_map(
        per_device,
        mesh=mesh,
        in_specs=(
            P(("grp", "shard"), None),
            P(("grp", "shard")),
            P(("grp", "shard")),
            P("grp", "shard", None),
            P("grp", None),
            P("grp", None),
            P("grp"),
            P("grp", "shard"),
        ),
        out_specs=P(("grp", "shard")),
        check_vma=False,
    )
```

```python
import functools

import jax
import jax.numpy as jnp
from jax import lax
from jax.experimental import pallas as pl
from jax.experimental.pallas import tpu as pltpu
from jax.sharding import PartitionSpec as P

MESH = pl.DeviceIdType.MESH
epsilon = 1e-06
DEAD = 2147483647
CH = 128
HALF = CH // 2

Q_ORDER = [
    (0, 0), (0, 3),
    (3, 0), (1, 0),
    (0, 1), (0, 2),
    (3, 3), (1, 3),
    (3, 1), (1, 1),
    (3, 2), (1, 2),
    (2, 0), (2, 3),
    (2, 1), (2, 2),
]
Q_SLOT = {place: i for i, place in enumerate(Q_ORDER)}
K_ORDER = [
    (0, 0, 0), (0, 0, 1), (0, 1, 0), (0, 1, 1),
    (0, 0, 2), (0, 0, 3), (0, 1, 2), (0, 1, 3),
]
J_ORDER = [0, 2, 1, 3]
for _j in J_ORDER:
    K_ORDER += [(3, 0, _j), (3, 1, _j), (1, 0, _j), (1, 1, _j)]
for _j in (0, 2):
    K_ORDER += [(2, 0, _j), (2, 1, _j), (2, 0, _j + 1), (2, 1, _j + 1)]
K_ROW = {
    place + (h,): i * CH + h * HALF if i < 28 else 28 * CH + h * 4 * HALF + (i - 28) * HALF
    for i, place in enumerate(K_ORDER)
    for h in range(2)
}
DY_ORDER = [0, 3, 1, 2]


def kernel(
    rows_hbm, ids_hbm, order_hbm, codes_hbm, scales_hbm, offsets_hbm, counts_hbm, key_order_hbm,
    out_ref,
    rows, ids_ref, order_ref, codes, scales_ref, offsets_ref, counts_ref, key_order_ref,
    sendq, sendo, qbuf, kbuf, qin, qord, kord, kob, acc, ans, perm,
    local_sem, send_sem, q_sem, k_sem, qo_sem, ko_sem, back_sem,
):
    y = lax.axis_index("grp")
    shard = lax.axis_index("shard")
    x, z, c = shard // 8, (shard // 2) % 4, shard % 2

    def device(dx=0, dy=0, dz=0, dc=0):
        return (
            (y + dy) % 4,
            (((x + dx) % 4) * 4 + (z + dz) % 4) * 2 + (c + dc) % 2,
        )

    started = []

    def send(src, dst, sem, to):
        copy = pltpu.make_async_remote_copy(
            src_ref=src,
            dst_ref=dst,
            send_sem=send_sem.at[len(started)],
            recv_sem=sem,
            device_id=to,
            device_id_type=MESH,
        )
        copy.start()
        started.append(copy)

    def arrived(dst, sem):
        pltpu.make_async_remote_copy(
            src_ref=dst,
            dst_ref=dst,
            send_sem=send_sem.at[0],
            recv_sem=sem,
            device_id=device(dc=1),
            device_id_type=MESH,
        ).wait_recv()

    def q_half(place, h):
        slot = Q_SLOT[place]
        return qbuf.at[pl.ds(slot * CH + h * HALF, HALF), :], q_sem.at[2 * slot + h]

    def k_part(place, h=None):
        row = K_ROW[place + (h or 0,)]
        return kbuf.at[pl.ds(row, CH if h is None else HALF), :], k_sem.at[row // HALF]

    barrier = pltpu.get_barrier_semaphore()
    near = [{"dx": 1}, {"dx": 3}, {"dy": 1}, {"dy": 2}, {"dy": 3}, {"dz": 1}, {"dz": 3}, {"dc": 1}]
    for place in near:
        pl.semaphore_signal(barrier, inc=1, device_id=device(**place), device_id_type=MESH)


    loads = [
        pltpu.make_async_copy(src, dst, local_sem.at[i])
        for i, (src, dst) in enumerate(
            (
                (scales_hbm, scales_ref),
                (offsets_hbm, offsets_ref),
                (codes_hbm.at[pl.ds(0, CH), :], codes.at[pl.ds(0, CH), :]),
                (counts_hbm, counts_ref),
                (key_order_hbm, key_order_ref),
                (ids_hbm, ids_ref),
                (order_hbm, order_ref),
                (rows_hbm, rows),
                *((codes_hbm.at[pl.ds(j * CH, CH), :], codes.at[pl.ds(j * CH, CH), :]) for j in J_ORDER[1:]),
            )
        )
    ]
    for load in loads:
        load.start()

    def decode(i):
        j = J_ORDER[i]
        if i:
            loads[7 + i].wait()
        decoded = (
            codes[pl.ds(j * CH, CH), :].astype(jnp.float32) * scales_ref[j // 2 : j // 2 + 1, :]
            + offsets_ref[j // 2 : j // 2 + 1, :]
        )
        kbuf[pl.ds(K_ROW[0, 0, j, 0], CH), :] = (
            decoded * lax.rsqrt(jnp.sum(decoded * decoded, axis=-1, keepdims=True) + epsilon)
        ).astype(jnp.bfloat16)

    def spread(j):
        here, _ = k_part((0, 0, j))
        for to, place in (
            (device(dz=1), (3, 0, j)),
            (device(dz=3), (1, 0, j)),
            (device(dc=1), (0, 1, j)),
        ):
            send(here, *k_part(place), to)

    def keys_order(dz, dc):
        return kord.at[dc * 4 + dz], ko_sem.at[dc * 4 + dz]

    for load in loads[:5]:
        load.wait()
    for j in range(4):
        place = shard * 256 + (j % 2) * CH + lax.broadcasted_iota(jnp.int32, (1, CH), 1)
        live = place < counts_ref[j // 2]
        kord[0, j : j + 1, :] = jnp.where(
            live, key_order_ref[j // 2 : j // 2 + 1, (j % 2) * CH : (j % 2 + 1) * CH], DEAD
        )

    decode(0)

    pl.semaphore_wait(barrier, len(near))

    here, _ = keys_order(0, 0)
    send(here, *keys_order(3, 0), device(dz=1))
    send(here, *keys_order(1, 0), device(dz=3))
    send(here, *keys_order(0, 1), device(dc=1))
    spread(J_ORDER[0])

    n_rows = rows.shape[0]
    for load in loads[5:7]:
        load.wait()
    ids = ids_ref[...]
    target = (ids // 2 - y + 4) % 4
    groups = lax.broadcasted_iota(jnp.int32, (16, n_rows), 0)
    onehot = jnp.where(groups == target, 1.0, 0.0)
    before = lax.broadcasted_iota(jnp.int32, (n_rows, n_rows), 0) < lax.broadcasted_iota(
        jnp.int32, (n_rows, n_rows), 1
    )
    earlier = jnp.dot(
        onehot.astype(jnp.bfloat16),
        jnp.where(before, 1.0, 0.0).astype(jnp.bfloat16),
        preferred_element_type=jnp.float32,
    )
    position = jnp.sum(
        onehot * (earlier + (groups * CH).astype(jnp.float32)), axis=0, keepdims=True
    ).astype(jnp.int32)
    slots = lax.broadcasted_iota(jnp.int32, (4 * CH, n_rows), 0)
    perm[...] = jnp.where(slots == position, 1.0, 0.0).astype(jnp.bfloat16)

    order = order_ref[...]
    pieces = []
    for cluster in range(2):
        own = jnp.where(ids % 2 == cluster, order, 0)
        pieces += [(own >> (8 * p)) & 255 for p in range(4)]
    pieces = jnp.concatenate(pieces + pieces, axis=0).astype(jnp.float32).astype(jnp.bfloat16)
    moved = lax.dot_general(
        pieces, perm[...], (((1,), (1,)), ((), ())), preferred_element_type=jnp.float32
    ).astype(jnp.int32)
    for d in range(4):
        for cluster in range(2):
            part = moved[4 * cluster : 4 * cluster + 4, d * CH : (d + 1) * CH]
            joined = part[0:1] + part[1:2] * 256 + part[2:3] * 65536 + part[3:4] * 16777216
            if d == 0:
                qin[0, 0, cluster : cluster + 1, :] = joined
            else:
                sendo[d, cluster : cluster + 1, :] = joined
    loads[7].wait()
    values = rows[...].astype(jnp.float32)
    queries = (
        values * lax.rsqrt(jnp.sum(values * values, axis=-1, keepdims=True) + epsilon)
    ).astype(jnp.bfloat16)

    def picked(d):
        return jnp.dot(
            perm[pl.ds(d * CH, CH), :], queries, preferred_element_type=jnp.float32
        ).astype(jnp.bfloat16)

    def send_x(dy, h):
        here, _ = q_half((0, dy), h)
        for dx, there in ((1, 3), (3, 1)):
            send(here, *q_half((there, dy), h), device(dx=dx))

    def send_y(d, h):
        send(sendq.at[d, pl.ds(h * HALF, HALF)], *q_half((0, (4 - d) % 4), h), device(dy=d))

    for d in range(1, 4):
        send(sendo.at[d], qin.at[0, 4 - d], qo_sem.at[0], device(dy=d))
    qbuf[pl.ds(0, CH), :] = picked(0)
    for h in range(2):
        send_x(0, h)
    for d in (1, 3):
        sendq[d] = picked(d)
    for h in range(2):
        for d in (1, 3):
            send_y(d, h)
    sendq[2] = picked(2)
    for i in range(1, 4):
        decode(i)
        spread(J_ORDER[i])

    arrived(qin.at[0, pl.ds(1, 3)], qo_sem.at[0])
    send(qin.at[0], qin.at[3], qo_sem.at[3], device(dx=1))
    send(qin.at[0], qin.at[1], qo_sem.at[1], device(dx=3))
    for dz in (3, 1):
        arrived(*keys_order(dz, 0))
        send(keys_order(dz, 0)[0], *keys_order(dz, 1), device(dc=1))
    send(keys_order(3, 0)[0], *keys_order(2, 0), device(dz=1))

    def spread_orders(dz, dc):
        for j in range(4):
            turned = jnp.broadcast_to(kord[dc * 4 + dz, j : j + 1, :], (CH, CH)).T
            for h in range(2):
                kob[pl.ds(K_ROW[dz, dc, j, h], HALF), :] = turned[h * HALF : (h + 1) * HALF]

    def place_orders(dx):
        for dy in range(4):
            qord[Q_SLOT[dx, dy]] = qin[dx, dy]

    acc[...] = jnp.zeros_like(acc)
    place_orders(0)
    for dz in (0, 3, 1):
        spread_orders(dz, 0)
        arrived(*keys_order(dz, 1))
        spread_orders(dz, 1)

    def tile(key_row, n_keys, block, n_blocks):
        keys = kbuf[pl.ds(pl.multiple_of(key_row, 2 * CH), n_keys), :]
        asks = qbuf[pl.ds(pl.multiple_of(block * CH, CH), n_blocks * CH), :]
        return lax.dot_general(
            keys, asks, (((1,), (1,)), ((), ())), preferred_element_type=jnp.float32
        )

    def keep(key_row, n_keys, block, n_blocks, scores):
        key_order = kob[pl.ds(pl.multiple_of(key_row, 2 * CH), n_keys), :]
        cluster = (key_row // (4 * CH)) % 2
        for h in range(n_blocks):
            limit = qord[block + h, pl.ds(cluster, 1), :]
            part = jnp.where(key_order < limit, scores[:, h * CH : (h + 1) * CH], 0.0)
            best = jnp.max(part.reshape(n_keys // 8, 8, CH), axis=0)
            acc[block + h] = jnp.maximum(acc[block + h], best)

    def tiles(*items):
        scores = [tile(*item) for item in items]
        for item, found in zip(items, scores):
            keep(*item, found)

    def work(count, place, n_keys, n_blocks, together):
        def some(first, size):
            at = [place(first + i) for i in range(size)]
            scores = [tile(row, n_keys, block, n_blocks) for row, block in at]
            for (row, block), found in zip(at, scores):
                keep(row, n_keys, block, n_blocks, found)

        def step(i, carry):
            some(together * i, together)
            return carry

        lax.fori_loop(0, count // together, step, 0)
        if count % together:
            some(count - count % together, count % together)

    def new_queries(qt, n_qt, n_kt):
        work(
            n_kt * n_qt, lambda i: ((i % n_kt) * 4 * CH, (qt + i // n_kt) * 2), 4 * CH, 2, 2
        )

    def new_keys(row, n_keys, n_qt):
        work(n_qt // 2, lambda i: (row, i * 4), n_keys, 4, 1)
        if n_qt % 2:
            work(1, lambda i: (row, (n_qt - 1) * 2), n_keys, 2, 1)

    def other_core(place, h=None):
        dz, _, j = place
        send(k_part(place, h)[0], *k_part((dz, 1, j), h), device(dc=1))

    def got_keys(*places, h=None):
        for place in places:
            arrived(*k_part(place, h))

    def got_queries(place, h):
        arrived(*q_half(place, h))

    def give_back(places):
        for dx, dy in sorted(places, key=lambda p: -(min(p[0], 4 - p[0]) + min(p[1], 4 - p[1]))):
            slot = Q_SLOT[(4 - dx) % 4, (4 - dy) % 4]
            send(acc.at[Q_SLOT[dx, dy]], ans.at[slot], back_sem.at[0], device(dx=dx, dy=dy))

    for tick in range(1, 7):
        if tick <= 4:
            j, dy = J_ORDER[tick - 1], DY_ORDER[tick - 1]
            if tick == 1:
                for ready in (3, 1):
                    for h in range(2):
                        got_queries((0, ready), h)
                        send_x(ready, h)
            if tick == 1:
                for h in range(2):
                    send_y(2, h)
            got_keys((3, 0, j), (1, 0, j))
            side, to = ((3, 1), (1, 3))[j % 2]
            if j < 2:
                send(k_part((side, 0, j))[0], *k_part((2, 0, j)), device(dz=to))
            else:
                for h in range(2):
                    row = K_ROW[side, 0, j, h]
                    send(kbuf.at[pl.ds(row, HALF), :], *k_part((2, 0, j), h), device(dz=to))
            other_core((3, 0, j))
            other_core((1, 0, j))
            if tick == 2:
                for h in range(2):
                    got_queries((0, 2), h)
                    send_x(2, h)
            for h in range(2):
                got_queries((3, dy), h)
                got_queries((1, dy), h)
            for passed in {2: (0, 3), 3: (1,), 4: (2,)}.get(tick, ()):
                side, to = (3, 1) if passed in (0, 1) else (1, 3)
                for h in range(2):
                    send(
                        q_half((side, passed), h)[0], *q_half((2, passed), h), device(dx=to)
                    )
            if tick == 1:
                for dx in (3, 1):
                    arrived(qin.at[dx], qo_sem.at[dx])
                    place_orders(dx)
                send(qin.at[3], qin.at[2], qo_sem.at[2], device(dx=1))
                got_keys(*((0, 1, own) for own in J_ORDER))
                new_queries(0, 2, 2)
                n_q = 2
            elif tick == 2:
                new_queries(2, 2, 3)
                n_q = 4
            else:
                new_queries(tick + 1, 1, tick + 1)
                n_q = tick + 2
            got_keys((3, 1, j), (1, 1, j))
            if tick == 4:
                arrived(*keys_order(2, 0))
                send(keys_order(2, 0)[0], *keys_order(2, 1), device(dc=1))
            new_keys((tick + 1) * 4 * CH, 4 * CH, n_q)
            if tick == 4:
                arrived(qin.at[2], qo_sem.at[2])
                place_orders(2)
                spread_orders(2, 0)
                arrived(*keys_order(2, 1))
                spread_orders(2, 1)
        elif tick == 5:
            got_keys((2, 0, 0), (2, 0, 1))
            other_core((2, 0, 0))
            other_core((2, 0, 1))
            for dy in (0, 3):
                for h in range(2):
                    got_queries((2, dy), h)
            tiles(*((kt * 4 * CH, 4 * CH, 12, 2) for kt in range(6)))
            got_keys((2, 1, 0), (2, 1, 1))
            tiles((6 * 4 * CH, 4 * CH, 0, 8))
            got_keys((2, 0, 2), (2, 0, 3), h=0)
            other_core((2, 0, 2), 0)
            other_core((2, 0, 3), 0)
            tiles((6 * 4 * CH, 4 * CH, 8, 6))
        else:
            last = 7 * 4 * CH
            got_keys((2, 1, 2), (2, 1, 3), h=0)
            tiles((last, 2 * CH, 0, 14))
            got_keys((2, 0, 2), (2, 0, 3), h=1)
            other_core((2, 0, 2), 1)
            other_core((2, 0, 3), 1)
            for dy in (1, 2):
                for h in range(2):
                    got_queries((2, dy), h)
            tiles(
                *((kt * 4 * CH, 4 * CH, 14, 2) for kt in range(7)), (last, 2 * CH, 14, 2)
            )
            got_keys((2, 1, 2), (2, 1, 3), h=1)
            tiles((last + 2 * CH, 2 * CH, 8, 8))
            give_back(Q_ORDER[:7:-1])
            tiles((last + 2 * CH, 2 * CH, 0, 8))
            give_back(Q_ORDER[1:8])

    for copy in started[:-15]:
        copy.wait_send()
    arrived(ans.at[pl.ds(1, 15)], back_sem.at[0])
    answers = []
    for d in range(4):
        best = acc[0] if d == 0 else ans[Q_SLOT[0, d]]
        for dx in range(1, 4):
            best = jnp.maximum(best, ans[Q_SLOT[dx, d]])
        answers.append(jnp.max(best, axis=0, keepdims=True))
    answer = jnp.concatenate(answers, axis=1)
    high = answer.astype(jnp.bfloat16).astype(jnp.float32)
    middle = (answer - high).astype(jnp.bfloat16).astype(jnp.float32)
    low = answer - high - middle
    parts = jnp.concatenate([high, middle, low, jnp.zeros((13, 4 * CH), jnp.float32)], axis=0)
    back = jnp.dot(parts.astype(jnp.bfloat16), perm[...], preferred_element_type=jnp.float32)
    out_ref[...] = back[0:8]
    for copy in started[-15:]:
        copy.wait_send()


def per_device(new_rows, cluster_ids, new_order, codes, scales, offsets, counts, earlier_order):
    n_rows, width = new_rows.shape
    vmem = pl.BlockSpec(memory_space=pltpu.VMEM)
    n_q, n_k = len(Q_ORDER), len(K_ORDER)
    out = pl.pallas_call(
        kernel,
        out_shape=jax.ShapeDtypeStruct((8, n_rows), jnp.float32),
        in_specs=[pl.BlockSpec(memory_space=pl.ANY)] * 8,
        out_specs=vmem,
        scratch_shapes=[
            pltpu.VMEM((n_rows, width), jnp.bfloat16),
            pltpu.VMEM((1, n_rows), jnp.int32),
            pltpu.VMEM((1, n_rows), jnp.int32),
            pltpu.VMEM((4 * CH, width), jnp.bfloat16),
            pltpu.VMEM((2, width), jnp.float32),
            pltpu.VMEM((2, width), jnp.float32),
            pltpu.SMEM((2,), jnp.int32),
            pltpu.VMEM((2, 2 * CH), jnp.int32),
            pltpu.VMEM((4, CH, width), jnp.bfloat16),
            pltpu.VMEM((4, 2, CH), jnp.int32),
            pltpu.VMEM((n_q * CH, width), jnp.bfloat16),
            pltpu.VMEM((n_k * CH, width), jnp.bfloat16),
            pltpu.VMEM((4, 4, 2, CH), jnp.int32),
            pltpu.VMEM((n_q, 2, CH), jnp.int32),
            pltpu.VMEM((8, 4, CH), jnp.int32),
            pltpu.VMEM((n_k * CH, CH), jnp.int32),
            pltpu.VMEM((n_q, 8, CH), jnp.float32),
            pltpu.VMEM((n_q, 8, CH), jnp.float32),
            pltpu.VMEM((4 * CH, n_rows), jnp.bfloat16),
            pltpu.SemaphoreType.DMA((11,)),
            pltpu.SemaphoreType.DMA((128,)),
            pltpu.SemaphoreType.DMA((2 * n_q,)),
            pltpu.SemaphoreType.DMA((2 * n_k,)),
            pltpu.SemaphoreType.DMA((4,)),
            pltpu.SemaphoreType.DMA((8,)),
            pltpu.SemaphoreType.DMA((1,)),
        ],
        compiler_params=pltpu.CompilerParams(
            collective_id=0, has_side_effects=True, vmem_limit_bytes=63 * 2**20
        ),
        cost_estimate=pl.CostEstimate(
            flops=2 * n_q * n_k * CH * CH * width, bytes_accessed=2**21, transcendentals=1024
        ),
    )(
        new_rows,
        cluster_ids.reshape(1, n_rows),
        new_order.reshape(1, n_rows),
        codes.reshape(4 * CH, width),
        scales,
        offsets,
        counts,
        earlier_order,
    )
    return out[0] + out[1] + out[2]


def solution(mesh):
    return jax.shard_map(
        per_device,
        mesh=mesh,
        in_specs=(
            P(("grp", "shard"), None),
            P(("grp", "shard")),
            P(("grp", "shard")),
            P("grp", "shard", None),
            P("grp", None),
            P("grp", None),
            P("grp"),
            P("grp", "shard"),
        ),
        out_specs=P(("grp", "shard")),
        check_vma=False,
    )
```
